1024 devices in a mesh: dp: 128 (over y_lo, x, z), tensor: 8 (over y_hi, core).
Axes of the slice: x: 4, y: 8 (y_hi: 4, y_lo: 2; y = y_hi * 2 + y_lo), z: 16, core: 2. Of those that a mesh axis runs over, the one named last changes fastest.
Arguments:
- attn: bfloat16 [16384, 3072], P('dp', 'tensor'), may hold values from -6 to 6
- weight: bfloat16 [2560, 3072], P(None, 'tensor'), may hold values from -0.109375 to 0.109375
- d_out: bfloat16 [16384, 2560], P(('dp', 'tensor')), may hold values from -24 to 24
Outputs:
- mixed: bfloat16 [16384, 2560], P(('dp', 'tensor'))
- d_attn: bfloat16 [16384, 3072], P('dp', 'tensor')
- w_grad: float32 [2560, 3072], P('dp', 'tensor')
The draws below stay inside these ranges and needn't reach their ends.
All inputs are finite; a program needn't handle non-finite values. Where the reference program divides by a largest or mean magnitude, that divisor is 1e-20 or more.
Results may differ from the reference program's by a relative error of at most 0.035.
The reference program's roundings to bfloat16 on the way (of `scale` and `coded`) count: a program that leaves them out, or rounds other values in their place, can miss the bound.
Values may be sent and summed in bfloat16 or wider, within the bound.
No kernel may reach another device: no remote copies, remote signals or barrier semaphores. Data moves between devices by JAX's collectives and lax.ppermute only.
A program may use at most 32 MiB of HBM per device.

```python
import jax
import jax.numpy as jnp
from jax import lax

HD = 128
HEADS_DEV = 3
DW = 2560
BLK = 128
GROUPS = 8
HEADS = 24
TOKENS = 16384


def strengthened(array, key, source, target, blocks, factor):
    def block_of(axis_at):
        return (jnp.arange(array.shape[axis_at]) // (array.shape[axis_at] // blocks)).reshape((-1,) + (1,) * (array.ndim - 1 - axis_at))

    first = jax.random.permutation(key, blocks)[block_of(target)]
    other_side = (block_of(target) + blocks // 2) % blocks
    return jnp.where((block_of(source) == first) | (block_of(source) == other_side), factor * array, array)


def block_levels(own_key, dims, split, least, top_value):
    gain, own = 1.0, jax.random.fold_in(own_key, 6)
    for position, shards_of in split:
        heights = jnp.exp(jax.random.uniform(jax.random.fold_in(own, position), (shards_of,), jnp.float32, least / len(split), top_value / len(split)))
        gain = gain * jnp.repeat(heights, dims[position] // shards_of).reshape([-1 if axis == position else 1 for axis in range(len(dims))])
    return gain


def noise(key, shape, deviation, bound, cuts=(), dtype=jnp.bfloat16):
    level = block_levels(key, shape, cuts, -0.22, 0.18) if cuts else 1.0
    drawn = jax.random.normal(key, shape, jnp.float32) * deviation * level
    return jnp.minimum(jnp.maximum(drawn, -bound), bound).astype(dtype)


def bell_draw_with(stream_key, shape, deviation, bound, split, heavy, dtype=jnp.bfloat16):
    entries = deviation * jax.random.normal(stream_key, shape, jnp.float32)
    if split:
        entries = entries * block_levels(stream_key, shape, split, -0.22, 0.18)
    return jnp.clip(strengthened(entries, jax.random.fold_in(stream_key, 3), *heavy), -bound, bound).astype(dtype)


def setup_inputs(seed: int = 0) -> dict:
    key_of = jax.random.split(jax.random.key(seed), 4)
    return {
        "attn": noise(key_of[0], (TOKENS, HEADS * HD), 1.0, 6.0, ((0, 128), (1, 8))),
        "weight": noise(key_of[1], (DW, HEADS * HD), (HEADS * HD) ** -0.5, 0.109375, ((1, 8),)),
        "d_out": bell_draw_with(key_of[2], (TOKENS, DW), 1.0, 24.0, ((0, 1024),), (0, 1, 512, 6.0)),
    }


code_offset = 6.0

def hadamard(size):
    rows = lax.broadcasted_iota(jnp.int32, (size, size), 0)
    cols = lax.broadcasted_iota(jnp.int32, (size, size), 1)
    common = jnp.bitwise_and(rows, cols)
    parity = jnp.zeros((size, size), jnp.int32)
    for place in range(size.bit_length() - 1):
        parity = parity + jnp.bitwise_and(jnp.right_shift(common, place), 1)
    signs = (1 - 2 * (parity % 2)).astype(jnp.float32)
    return signs / jnp.sqrt(jnp.float32(size))

def rotate(field, table):
    count = field.shape[0]
    blocks = field.reshape(count, -1, BLK)
    turned = jnp.einsum('rkb,bc->rkc', blocks, table, precision=lax.Precision.HIGHEST)
    return turned.reshape(count, -1)

def reference(attn, weight, d_out):
    table = hadamard(BLK)
    width = HEADS_DEV * HD
    count = attn.shape[0]
    total = jnp.zeros((count, weight.shape[0]), jnp.float32)
    for group in range(GROUPS):
        left = attn[:, group * width:(group + 1) * width]
        right = weight[:, group * width:(group + 1) * width]
        partial_value = lax.dot_general(left, right, (((1,), (1,)), ((), ())), preferred_element_type=jnp.float32)
        blocks = rotate(partial_value, table).reshape(count, -1, BLK)
        scale = (lax.optimization_barrier(jnp.max(jnp.abs(blocks), axis=2)) + 1e-06).astype(jnp.bfloat16).astype(jnp.float32)
        coded = lax.optimization_barrier((blocks / scale[:, :, None] + code_offset).astype(jnp.bfloat16))
        total = total + ((coded.astype(jnp.float32) - code_offset) * scale[:, :, None]).reshape(count, -1)
    mixed = rotate(total, table).astype(jnp.bfloat16)
    d_attn = jnp.dot(d_out, weight, preferred_element_type=jnp.float32).astype(jnp.bfloat16)
    w_grad = lax.dot_general(d_out, attn, (((0,), (0,)), ((), ())), preferred_element_type=jnp.float32)
    return (mixed, d_attn, w_grad)
```

```python
import jax
import jax.numpy as jnp
from jax import lax
from jax.sharding import Mesh
from jax.sharding import PartitionSpec as P

BLK = 128
TENSOR = ("yh", "core")
NEAR = ("yl", "x")
FAR = "z"

code_offset = 6.0


def hadamard(size):
    rows = lax.broadcasted_iota(jnp.int32, (size, size), 0)
    cols = lax.broadcasted_iota(jnp.int32, (size, size), 1)
    common = jnp.bitwise_and(rows, cols)
    parity = jnp.zeros((size, size), jnp.int32)
    for place in range(size.bit_length() - 1):
        parity = parity + jnp.bitwise_and(jnp.right_shift(common, place), 1)
    signs = (1 - 2 * (parity % 2)).astype(jnp.float32)
    return signs / jnp.sqrt(jnp.float32(size))


def rotate(field, table):
    count = field.shape[0]
    blocks = field.reshape(count, -1, BLK)
    turned = jnp.einsum("rkb,bc->rkc", blocks, table, precision=lax.Precision.HIGHEST)
    return turned.reshape(count, -1)


def body(attn, weight, d_out):
    table = hadamard(BLK)
    count = attn.shape[0]
    features, width = weight.shape
    partial_value = lax.dot_general(
        attn, weight, (((1,), (1,)), ((), ())), preferred_element_type=jnp.float32
    )
    blocks = rotate(partial_value, table).reshape(count, -1, BLK)
    scale = (jnp.max(jnp.abs(blocks), axis=2) + 1e-06).astype(jnp.bfloat16)
    coded = (blocks / scale.astype(jnp.float32)[:, :, None] + code_offset).astype(jnp.bfloat16)
    kept = lax.optimization_barrier(coded)
    values = (
        (kept.astype(jnp.float32) - code_offset) * scale.astype(jnp.float32)[:, :, None]
    ).reshape(count, features)
    total = lax.psum_scatter(
        values.astype(jnp.bfloat16), TENSOR, scatter_dimension=0, tiled=True
    ).astype(jnp.float32)
    mixed = rotate(total, table).astype(jnp.bfloat16)

    full_grad = lax.all_gather(d_out, TENSOR, axis=0, tiled=True)
    d_attn = jnp.dot(full_grad, weight, preferred_element_type=jnp.float32).astype(jnp.bfloat16)

    term = lax.dot_general(
        full_grad, attn, (((0,), (0,)), ((), ())), preferred_element_type=jnp.float32
    ).astype(jnp.bfloat16)
    near = lax.axis_size(NEAR)
    pieces = lax.all_to_all(term.reshape(near, features // near, width), NEAR, 0, 0)
    plane = jnp.sum(pieces.astype(jnp.float32), axis=0).astype(jnp.bfloat16)
    far = lax.axis_size(FAR)
    pieces = lax.all_to_all(plane.reshape(far, features // near // far, width), FAR, 0, 0)
    w_grad = jnp.sum(pieces.astype(jnp.float32), axis=0)
    return (mixed, d_attn, w_grad)


def solution(mesh):
    fine = Mesh(mesh.devices.reshape(2, 4, 16, 4, 2), ("yl", "x", "z", "yh", "core"))
    dp = ("yl", "x", "z")
    in_specs = (P(dp, TENSOR), P(None, TENSOR), P(dp + TENSOR, None))
    out_specs = (P(dp + TENSOR, None), P(dp, TENSOR), P(dp, TENSOR))
    return jax.shard_map(body, mesh=fine, in_specs=in_specs, out_specs=out_specs, check_vma=False)
```

```python
import functools

import jax
import jax.numpy as jnp
from jax import lax
from jax.sharding import Mesh
from jax.sharding import PartitionSpec as P

BLK = 128
TENSOR = ("yh", "core")
NEAR = ("yl", "x")
FAR = "z"

code_offset = 6.0


def hadamard(size):
    rows = lax.broadcasted_iota(jnp.int32, (size, size), 0)
    cols = lax.broadcasted_iota(jnp.int32, (size, size), 1)
    common = jnp.bitwise_and(rows, cols)
    parity = jnp.zeros((size, size), jnp.int32)
    for place in range(size.bit_length() - 1):
        parity = parity + jnp.bitwise_and(jnp.right_shift(common, place), 1)
    signs = (1 - 2 * (parity % 2)).astype(jnp.float32)
    return signs / jnp.sqrt(jnp.float32(size))


def rotate(field, table):
    count = field.shape[0]
    blocks = field.reshape(count, -1, BLK)
    turned = jnp.einsum("rkb,bc->rkc", blocks, table, precision=lax.Precision.HIGHEST)
    return turned.reshape(count, -1)


def coded_values(attn, weight, table):
    count, features = attn.shape[0], weight.shape[0]
    partial_value = lax.dot_general(
        attn, weight, (((1,), (1,)), ((), ())), preferred_element_type=jnp.float32
    )
    blocks = rotate(partial_value, table).reshape(count, -1, BLK)
    scale = (jnp.max(jnp.abs(blocks), axis=2) + 1e-06).astype(jnp.bfloat16)
    coded = (blocks / scale.astype(jnp.float32)[:, :, None] + code_offset).astype(jnp.bfloat16)
    kept = lax.optimization_barrier(coded)
    values = (kept.astype(jnp.float32) - code_offset) * scale.astype(jnp.float32)[:, :, None]
    return values.reshape(count, features).astype(jnp.bfloat16)


def scatter_sum(values):
    count, features = values.shape
    tall, cores = lax.axis_size("yh"), lax.axis_size("core")
    me, mine = lax.axis_index("yh"), lax.axis_index("core")
    view = values.reshape(tall, cores, count // tall // cores, features)
    pick = functools.partial(lax.dynamic_index_in_dim, keepdims=False)
    arrived = lax.ppermute(pick(view, 1 - mine, 1), "core", [(0, 1), (1, 0)])
    pair = pick(view, mine, 1).astype(jnp.float32) + arrived.astype(jnp.float32)
    sent = pair.astype(jnp.bfloat16)
    total = pick(pair, me, 0)
    for step in range(1, tall):
        block = pick(sent, lax.rem(me + step, tall), 0)
        arrived = lax.ppermute(block, "yh", [(i, (i + step) % tall) for i in range(tall)])
        total = total + arrived.astype(jnp.float32)
    return total


def body(attn, weight, d_out):
    table = hadamard(BLK)
    features, width = weight.shape
    full_grad = lax.all_gather(d_out, TENSOR, axis=0, tiled=True)

    term = lax.dot_general(
        full_grad, attn, (((0,), (0,)), ((), ())), preferred_element_type=jnp.float32
    ).astype(jnp.bfloat16)
    near = lax.axis_size(NEAR)
    pieces = lax.all_to_all(term.reshape(near, features // near, width), NEAR, 0, 0)
    pieces, attn, full_grad = lax.optimization_barrier((pieces, attn, full_grad))
    plane = jnp.sum(pieces.astype(jnp.float32), axis=0).astype(jnp.bfloat16)
    far = lax.axis_size(FAR)
    pieces = lax.all_to_all(plane.reshape(far, features // near // far, width), FAR, 0, 0)
    w_grad = jnp.sum(pieces.astype(jnp.float32), axis=0)

    total = scatter_sum(coded_values(attn, weight, table))
    mixed = rotate(total, table).astype(jnp.bfloat16)
    d_attn = jnp.dot(full_grad, weight, preferred_element_type=jnp.float32).astype(jnp.bfloat16)
    return (mixed, d_attn, w_grad)


def solution(mesh):
    fine = Mesh(mesh.devices.reshape(2, 4, 16, 4, 2), ("yl", "x", "z", "yh", "core"))
    dp = ("yl", "x", "z")
    in_specs = (P(dp, TENSOR), P(None, TENSOR), P(dp + TENSOR, None))
    out_specs = (P(dp + TENSOR, None), P(dp, TENSOR), P(dp, TENSOR))
    return jax.shard_map(body, mesh=fine, in_specs=in_specs, out_specs=out_specs, check_vma=False)
```

```python
import jax
import jax.numpy as jnp
from jax import lax
from jax.experimental import pallas as pl
from jax.experimental.pallas import tpu as pltpu
from jax.sharding import Mesh
from jax.sharding import PartitionSpec as P

BLK = 128
TENSOR = ("yh", "core")
NEAR = ("yl", "x")
FAR = "z"
CHUNKS = 8
WINDOW = 384
VMEM_LIMIT = 40 * 1024 * 1024

code_offset = 6.0
bf16, f32 = jnp.bfloat16, jnp.float32


def call(kernel, outs, scalars, *arrays, flops=0):
    specs = [pl.BlockSpec(memory_space=pltpu.SMEM)] * len(scalars)
    specs += [pl.BlockSpec(memory_space=pltpu.VMEM)] * len(arrays)
    moved = sum(a.size * a.dtype.itemsize for a in tuple(arrays) + tuple(outs))
    return pl.pallas_call(
        kernel,
        out_shape=outs,
        in_specs=specs,
        out_specs=tuple(pl.BlockSpec(memory_space=pltpu.VMEM) for _ in outs),
        compiler_params=pltpu.CompilerParams(vmem_limit_bytes=VMEM_LIMIT),
        cost_estimate=pl.CostEstimate(flops=flops, bytes_accessed=moved, transcendentals=0),
    )(*[jnp.reshape(s, (1,)).astype(jnp.int32) for s in scalars], *arrays)


def signs_table():
    rows = lax.broadcasted_iota(jnp.int32, (BLK, BLK), 0)
    cols = lax.broadcasted_iota(jnp.int32, (BLK, BLK), 1)
    common = jnp.bitwise_and(rows, cols)
    parity = jnp.zeros((BLK, BLK), jnp.int32)
    for place in range(BLK.bit_length() - 1):
        parity = parity + jnp.bitwise_and(jnp.right_shift(common, place), 1)
    return (1 - 2 * jnp.bitwise_and(parity, 1)).astype(f32).astype(bf16)


def rotate(field, table):
    high = field.astype(bf16)
    rest = field - high.astype(f32)
    middle = rest.astype(bf16)
    low = (rest - middle.astype(f32)).astype(bf16)
    turned = jnp.dot(high, table, preferred_element_type=f32)
    turned += jnp.dot(middle, table, preferred_element_type=f32)
    turned += jnp.dot(low, table, preferred_element_type=f32)
    return turned * (BLK**-0.5)


def pack_kernel(attn_ref, d_ref, out_ref):
    count = attn_ref.shape[0]
    for i in range(CHUNKS):
        out_ref[i, :count, :] = attn_ref[...]
        start = i * 320 // BLK * BLK
        out_ref[i, count:, :] = d_ref[:, start : start + WINDOW]


def values_kernel(core_ref, attn_ref, weight_ref, keep_ref, send_ref):
    table = signs_table()
    count, features = attn_ref.shape[0], weight_ref.shape[0]
    tall, rows = keep_ref.shape[0], keep_ref.shape[1]
    first = core_ref[0] == 0
    for j in range(features // BLK):
        cols = slice(j * BLK, (j + 1) * BLK)
        partial_value = lax.dot_general(
            attn_ref[...], weight_ref[cols, :], (((1,), (1,)), ((), ())), preferred_element_type=f32
        )
        turned = rotate(partial_value, table)
        top = jnp.max(jnp.abs(turned), axis=1, keepdims=True) + 1e-06
        scale = top.astype(bf16).astype(f32)
        coded = (turned / scale + code_offset).astype(bf16)
        values = ((coded.astype(f32) - code_offset) * scale).reshape(tall, 2, rows, BLK)
        zero, one = values[:, 0], values[:, 1]
        keep_ref[:, :, cols] = jnp.where(first, zero, one).astype(bf16)
        send_ref[:, :, cols] = jnp.where(first, one, zero).astype(bf16)


def pair_kernel(me_ref, keep_ref, arrived_ref, own_ref, *sent_refs):
    tall = keep_ref.shape[0]
    me = me_ref[0]
    own_ref[...] = keep_ref[me].astype(f32) + arrived_ref[me].astype(f32)
    for step in range(1, tall):
        other = lax.rem(me + step, tall)
        total = keep_ref[other].astype(f32) + arrived_ref[other].astype(f32)
        sent_refs[step - 1][...] = total.astype(bf16)


def mixed_kernel(own_ref, a_ref, b_ref, c_ref, out_ref):
    table = signs_table()
    for j in range(out_ref.shape[1] // BLK):
        cols = slice(j * BLK, (j + 1) * BLK)
        total = own_ref[:, cols] + a_ref[:, cols].astype(f32)
        total += b_ref[:, cols].astype(f32) + c_ref[:, cols].astype(f32)
        out_ref[:, cols] = rotate(total, table).astype(bf16)


def grad_kernel(odd_ref, near_ref, d_ref, out_ref):
    near, group, rows = d_ref.shape[1], d_ref.shape[0], d_ref.shape[2]
    count = group * rows
    left = jnp.concatenate([d_ref[:, p].reshape(count, WINDOW) for p in range(near)], axis=0)
    right = jnp.concatenate([near_ref[p, :count, :] for p in range(near)], axis=0)
    term = lax.dot_general(left, right, (((0,), (0,)), ((), ())), preferred_element_type=f32)
    far, size = out_ref.shape[0], out_ref.shape[1]
    chunk = far * size
    term = jnp.where(odd_ref[0] == 1, term[WINDOW - chunk :, :], term[:chunk, :])
    for z in range(far):
        out_ref[z] = term[z * size : (z + 1) * size, :].astype(bf16)


def total_kernel(pieces_ref, out_ref):
    out_ref[...] = jnp.sum(pieces_ref[...].astype(f32), axis=0)


def shape(dims, dtype):
    return jax.ShapeDtypeStruct(dims, dtype)


def body(attn, weight, d_out):
    count, width = attn.shape
    features = weight.shape[0]
    group, near, far = lax.axis_size(TENSOR), lax.axis_size(NEAR), lax.axis_size(FAR)
    tall = lax.axis_size("yh")
    rows = count // group
    yh, core = lax.axis_index("yh"), lax.axis_index("core")
    odd = lax.rem(lax.axis_index("x"), 2)

    (packed,) = call(pack_kernel, (shape((near, count + rows, width), bf16),), (), attn, d_out)
    packed, attn = lax.optimization_barrier((packed, attn))
    pieces = lax.all_to_all(packed, NEAR, 0, 0)

    half = shape((tall, rows, features), bf16)
    keep, send = call(
        values_kernel, (half, half), (core,), attn, weight, flops=2 * count * features * (width + 3 * BLK)
    )
    arrived = lax.ppermute(send, "core", [(0, 1), (1, 0)])
    one = shape((rows, features), bf16)
    own, *sent = call(pair_kernel, (shape((rows, features), f32), one, one, one), (yh,), keep, arrived)

    pieces, own = lax.optimization_barrier((pieces, own))
    chunk = lax.all_gather(pieces[:, count:, :], TENSOR)
    (plane,) = call(
        grad_kernel,
        (shape((far, features // near // far, width), bf16),),
        (odd,),
        pieces,
        chunk,
        flops=2 * near * count * WINDOW * width,
    )
    plane, d_out, sent = lax.optimization_barrier((plane, d_out, sent))
    terms = lax.all_to_all(plane, FAR, 0, 0)

    blocks = []
    for step in range(1, tall):
        blocks.append(lax.ppermute(sent[step - 1], "yh", [(i, (i + step) % tall) for i in range(tall)]))
    full_grad = lax.all_gather(d_out, TENSOR, axis=0, tiled=True)
    d_attn = jnp.dot(full_grad, weight, preferred_element_type=f32).astype(bf16)
    (mixed,) = call(mixed_kernel, (one,), (), own, *blocks)
    (w_grad,) = call(total_kernel, (shape((features // near // far, width), f32),), (), terms)
    return (mixed, d_attn, w_grad)


def solution(mesh):
    fine = Mesh(mesh.devices.reshape(2, 4, 16, 4, 2), ("yl", "x", "z", "yh", "core"))
    dp = ("yl", "x", "z")
    in_specs = (P(dp, TENSOR), P(None, TENSOR), P(dp + TENSOR, None))
    out_specs = (P(dp + TENSOR, None), P(dp, TENSOR), P(dp, TENSOR))
    return jax.shard_map(body, mesh=fine, in_specs=in_specs, out_specs=out_specs, check_vma=False)
```

```python
import jax
import jax.numpy as jnp
from jax import lax
from jax.experimental import pallas as pl
from jax.experimental.pallas import tpu as pltpu
from jax.sharding import Mesh
from jax.sharding import PartitionSpec as P

BLK = 128
TENSOR = ("yh", "core")
NEAR = ("yl", "x")
FAR = "z"
CHUNKS = 8
WINDOW = 384
VMEM_LIMIT = 40 * 1024 * 1024

code_offset = 6.0
bf16, f32 = jnp.bfloat16, jnp.float32


def call(kernel, outs, scalars, *arrays, flops=0):
    specs = [pl.BlockSpec(memory_space=pltpu.SMEM)] * len(scalars)
    specs += [pl.BlockSpec(memory_space=pltpu.VMEM)] * len(arrays)
    moved = sum(a.size * a.dtype.itemsize for a in tuple(arrays) + tuple(outs))
    return pl.pallas_call(
        kernel,
        out_shape=outs,
        in_specs=specs,
        out_specs=tuple(pl.BlockSpec(memory_space=pltpu.VMEM) for _ in outs),
        compiler_params=pltpu.CompilerParams(vmem_limit_bytes=VMEM_LIMIT),
        cost_estimate=pl.CostEstimate(flops=flops, bytes_accessed=moved, transcendentals=0),
    )(*[jnp.reshape(s, (1,)).astype(jnp.int32) for s in scalars], *arrays)


def signs_table():
    rows = lax.broadcasted_iota(jnp.int32, (BLK, BLK), 0)
    cols = lax.broadcasted_iota(jnp.int32, (BLK, BLK), 1)
    common = jnp.bitwise_and(rows, cols)
    parity = jnp.zeros((BLK, BLK), jnp.int32)
    for place in range(BLK.bit_length() - 1):
        parity = parity + jnp.bitwise_and(jnp.right_shift(common, place), 1)
    return (1 - 2 * jnp.bitwise_and(parity, 1)).astype(f32).astype(bf16)


def rotate(field, table):
    high = field.astype(bf16)
    rest = field - high.astype(f32)
    middle = rest.astype(bf16)
    low = (rest - middle.astype(f32)).astype(bf16)
    turned = jnp.dot(high, table, preferred_element_type=f32)
    turned += jnp.dot(middle, table, preferred_element_type=f32)
    turned += jnp.dot(low, table, preferred_element_type=f32)
    return turned * (BLK**-0.5)


def pack_kernel(attn_ref, d_ref, out_ref, sems):
    count = attn_ref.shape[0]
    copies = []
    for i in range(CHUNKS):
        start = i * 320 // BLK * BLK
        window = d_ref.at[:, pl.ds(start, WINDOW)]
        copies.append((attn_ref, out_ref.at[i, pl.ds(0, count), :]))
        copies.append((window, out_ref.at[i, pl.ds(count, d_ref.shape[0]), :]))
    copies = [pltpu.make_async_copy(a, b, sems.at[k]) for k, (a, b) in enumerate(copies)]
    for copy in copies:
        copy.start()
    for copy in copies:
        copy.wait()


def pack(attn, d_out):
    (count, width), rows = attn.shape, d_out.shape[0]
    out = shape((CHUNKS, count + rows, width), bf16)
    return pl.pallas_call(
        pack_kernel,
        out_shape=out,
        in_specs=[pl.BlockSpec(memory_space=pltpu.HBM)] * 2,
        out_specs=pl.BlockSpec(memory_space=pltpu.HBM),
        scratch_shapes=[pltpu.SemaphoreType.DMA((2 * CHUNKS,))],
        cost_estimate=pl.CostEstimate(flops=0, bytes_accessed=4 * out.size, transcendentals=0),
    )(attn, d_out)


def rows_kernel(near_ref, d_ref, out_ref):
    near, rows = near_ref.shape[0], d_ref.shape[0]
    for p in range(near):
        out_ref[:, p * WINDOW : (p + 1) * WINDOW] = near_ref[p, near_ref.shape[1] - rows :, :]
    out_ref[:, near * WINDOW :] = d_ref[...]


def values_kernel(core_ref, attn_ref, weight_ref, keep_ref, send_ref):
    table = signs_table()
    count, features = attn_ref.shape[0], weight_ref.shape[0]
    tall, rows = keep_ref.shape[0], keep_ref.shape[1]
    first = core_ref[0] == 0
    for j in range(features // BLK):
        cols = slice(j * BLK, (j + 1) * BLK)
        partial_value = lax.dot_general(
            attn_ref[...], weight_ref[cols, :], (((1,), (1,)), ((), ())), preferred_element_type=f32
        )
        turned = rotate(partial_value, table)
        top = jnp.max(jnp.abs(turned), axis=1, keepdims=True) + 1e-06
        scale = top.astype(bf16).astype(f32)
        coded = (turned / scale + code_offset).astype(bf16)
        values = ((coded.astype(f32) - code_offset) * scale).reshape(tall, 2, rows, BLK)
        zero, one = values[:, 0], values[:, 1]
        keep_ref[:, :, cols] = jnp.where(first, zero, one).astype(bf16)
        send_ref[:, :, cols] = jnp.where(first, one, zero).astype(bf16)


def pair_kernel(me_ref, keep_ref, arrived_ref, own_ref, *sent_refs):
    tall = keep_ref.shape[0]
    me = me_ref[0]
    own_ref[...] = keep_ref[me].astype(f32) + arrived_ref[me].astype(f32)
    for step in range(1, tall):
        other = lax.rem(me + step, tall)
        total = keep_ref[other].astype(f32) + arrived_ref[other].astype(f32)
        sent_refs[step - 1][...] = total.astype(bf16)


def mixed_kernel(own_ref, a_ref, b_ref, c_ref, out_ref):
    table = signs_table()
    for j in range(out_ref.shape[1] // BLK):
        cols = slice(j * BLK, (j + 1) * BLK)
        total = own_ref[:, cols] + a_ref[:, cols].astype(f32)
        total += b_ref[:, cols].astype(f32) + c_ref[:, cols].astype(f32)
        out_ref[:, cols] = rotate(total, table).astype(bf16)


def grad_kernel(odd_ref, near_ref, d_ref, out_ref):
    near, count = near_ref.shape[0], d_ref.shape[0]
    left = jnp.concatenate([d_ref[:, p * WINDOW : (p + 1) * WINDOW] for p in range(near)], axis=0)
    right = jnp.concatenate([near_ref[p, :count, :] for p in range(near)], axis=0)
    term = lax.dot_general(left, right, (((0,), (0,)), ((), ())), preferred_element_type=f32)
    far, size = out_ref.shape[0], out_ref.shape[1]
    chunk = far * size
    term = jnp.where(odd_ref[0] == 1, term[WINDOW - chunk :, :], term[:chunk, :])
    for z in range(far):
        out_ref[z] = term[z * size : (z + 1) * size, :].astype(bf16)


def d_attn_kernel(d_ref, weight_ref, out_ref):
    start = d_ref.shape[1] - weight_ref.shape[0]
    product = jnp.dot(d_ref[:, start:], weight_ref[...], preferred_element_type=f32)
    out_ref[...] = product.astype(bf16)


def total_kernel(pieces_ref, out_ref):
    out_ref[...] = jnp.sum(pieces_ref[...].astype(f32), axis=0)


def shape(dims, dtype):
    return jax.ShapeDtypeStruct(dims, dtype)


def body(attn, weight, d_out):
    count, width = attn.shape
    features = weight.shape[0]
    group, near, far = lax.axis_size(TENSOR), lax.axis_size(NEAR), lax.axis_size(FAR)
    tall = lax.axis_size("yh")
    rows = count // group
    yh, core = lax.axis_index("yh"), lax.axis_index("core")
    odd = lax.rem(lax.axis_index("x"), 2)

    packed = pack(attn, d_out)
    packed, attn = lax.optimization_barrier((packed, attn))
    pieces = lax.all_to_all(packed, NEAR, 0, 0)

    half = shape((tall, rows, features), bf16)
    keep, send = call(
        values_kernel, (half, half), (core,), attn, weight, flops=2 * count * features * (width + 3 * BLK)
    )
    arrived = lax.ppermute(send, "core", [(0, 1), (1, 0)])
    one = shape((rows, features), bf16)
    own, *sent = call(pair_kernel, (shape((rows, features), f32), one, one, one), (yh,), keep, arrived)

    pieces, own, d_out = lax.optimization_barrier((pieces, own, d_out))
    (lines,) = call(rows_kernel, (shape((rows, near * WINDOW + features), bf16),), (), pieces, d_out)
    lines = lax.all_gather(lines, TENSOR, axis=0, tiled=True)
    (plane,) = call(
        grad_kernel,
        (shape((far, features // near // far, width), bf16),),
        (odd,),
        pieces,
        lines,
        flops=2 * near * count * WINDOW * width,
    )
    plane, lines, sent = lax.optimization_barrier((plane, lines, sent))
    terms = lax.all_to_all(plane, FAR, 0, 0)

    blocks = []
    for step in range(1, tall):
        blocks.append(lax.ppermute(sent[step - 1], "yh", [(i, (i + step) % tall) for i in range(tall)]))
    (d_attn,) = call(
        d_attn_kernel, (shape((count, width), bf16),), (), lines, weight, flops=2 * count * features * width
    )
    (mixed,) = call(mixed_kernel, (one,), (), own, *blocks)
    (w_grad,) = call(total_kernel, (shape((features // near // far, width), f32),), (), terms)
    return (mixed, d_attn, w_grad)


def solution(mesh):
    fine = Mesh(mesh.devices.reshape(2, 4, 16, 4, 2), ("yl", "x", "z", "yh", "core"))
    dp = ("yl", "x", "z")
    in_specs = (P(dp, TENSOR), P(None, TENSOR), P(dp + TENSOR, None))
    out_specs = (P(dp + TENSOR, None), P(dp, TENSOR), P(dp, TENSOR))
    return jax.shard_map(body, mesh=fine, in_specs=in_specs, out_specs=out_specs, check_vma=False)
```

```python
import jax
import jax.numpy as jnp
from jax import lax
from jax.experimental import pallas as pl
from jax.experimental.pallas import tpu as pltpu
from jax.sharding import Mesh
from jax.sharding import PartitionSpec as P

BLK = 128
TENSOR = ("yh", "core")
NEAR = ("yl", "x")
FAR = "z"
CHUNKS = 8
WINDOW = 384
VMEM_LIMIT = 40 * 1024 * 1024

code_offset = 6.0
bf16, f32 = jnp.bfloat16, jnp.float32


def call(kernel, outs, scalars, *arrays, flops=0):
    specs = [pl.BlockSpec(memory_space=pltpu.SMEM)] * len(scalars)
    specs += [pl.BlockSpec(memory_space=pltpu.VMEM)] * len(arrays)
    moved = sum(a.size * a.dtype.itemsize for a in tuple(arrays) + tuple(outs))
    return pl.pallas_call(
        kernel,
        out_shape=outs,
        in_specs=specs,
        out_specs=tuple(pl.BlockSpec(memory_space=pltpu.VMEM) for _ in outs),
        compiler_params=pltpu.CompilerParams(vmem_limit_bytes=VMEM_LIMIT),
        cost_estimate=pl.CostEstimate(flops=flops, bytes_accessed=moved, transcendentals=0),
    )(*[jnp.reshape(s, (1,)).astype(jnp.int32) for s in scalars], *arrays)


def signs_table():
    rows = lax.broadcasted_iota(jnp.int32, (BLK, BLK), 0)
    cols = lax.broadcasted_iota(jnp.int32, (BLK, BLK), 1)
    common = jnp.bitwise_and(rows, cols)
    parity = jnp.zeros((BLK, BLK), jnp.int32)
    for place in range(BLK.bit_length() - 1):
        parity = parity + jnp.bitwise_and(jnp.right_shift(common, place), 1)
    return (1 - 2 * jnp.bitwise_and(parity, 1)).astype(f32).astype(bf16)


def rotate(field, table):
    high = field.astype(bf16)
    rest = field - high.astype(f32)
    middle = rest.astype(bf16)
    low = (rest - middle.astype(f32)).astype(bf16)
    turned = jnp.dot(high, table, preferred_element_type=f32)
    turned += jnp.dot(middle, table, preferred_element_type=f32)
    turned += jnp.dot(low, table, preferred_element_type=f32)
    return turned * (BLK**-0.5)


def pack_kernel(attn_ref, d_ref, out_ref):
    count = attn_ref.shape[0]
    for i in range(CHUNKS):
        start = i * 320 // BLK * BLK
        out_ref[i, :count, :] = attn_ref[...]
        out_ref[i, count:, :] = d_ref[:, start : start + WINDOW]


def values_kernel(core_ref, attn_ref, weight_ref, keep_ref, send_ref):
    table = signs_table()
    count, features = attn_ref.shape[0], weight_ref.shape[0]
    tall, rows = keep_ref.shape[0], keep_ref.shape[1]
    first = core_ref[0] == 0
    for j in range(features // BLK):
        cols = slice(j * BLK, (j + 1) * BLK)
        partial_value = lax.dot_general(
            attn_ref[...], weight_ref[cols, :], (((1,), (1,)), ((), ())), preferred_element_type=f32
        )
        turned = rotate(partial_value, table)
        top = jnp.max(jnp.abs(turned), axis=1, keepdims=True) + 1e-06
        scale = top.astype(bf16).astype(f32)
        coded = (turned / scale + code_offset).astype(bf16)
        values = ((coded.astype(f32) - code_offset) * scale).reshape(tall, 2, rows, BLK)
        zero, one = values[:, 0], values[:, 1]
        keep_ref[:, :, cols] = jnp.where(first, zero, one).astype(bf16)
        send_ref[:, :, cols] = jnp.where(first, one, zero).astype(bf16)


def pair_kernel(me_ref, keep_ref, arrived_ref, own_ref, *sent_refs):
    tall = keep_ref.shape[0]
    me = me_ref[0]
    own_ref[...] = keep_ref[me].astype(f32) + arrived_ref[me].astype(f32)
    for step in range(1, tall):
        other = lax.rem(me + step, tall)
        total = keep_ref[other].astype(f32) + arrived_ref[other].astype(f32)
        sent_refs[step - 1][...] = total.astype(bf16)


def mixed_kernel(own_ref, a_ref, b_ref, c_ref, out_ref):
    table = signs_table()
    for j in range(out_ref.shape[1] // BLK):
        cols = slice(j * BLK, (j + 1) * BLK)
        total = own_ref[:, cols] + a_ref[:, cols].astype(f32)
        total += b_ref[:, cols].astype(f32) + c_ref[:, cols].astype(f32)
        out_ref[:, cols] = rotate(total, table).astype(bf16)


def grad_kernel(odd_ref, near_ref, out_ref):
    near, count = near_ref.shape[0], near_ref.shape[1] // 2
    left = jnp.concatenate([near_ref[p, count:, :] for p in range(near)], axis=0)
    right = jnp.concatenate([near_ref[p, :count, :] for p in range(near)], axis=0)
    term = lax.dot_general(left, right, (((0,), (0,)), ((), ())), preferred_element_type=f32)
    far, size = out_ref.shape[0], out_ref.shape[1] * BLK // term.shape[1]
    chunk = far * size
    term = jnp.where(odd_ref[0] == 1, term[WINDOW - chunk :, :], term[:chunk, :])
    for z in range(far):
        block = term[z * size : (z + 1) * size, :]
        parts = [block[:, c : c + BLK] for c in range(0, term.shape[1], BLK)]
        out_ref[z] = jnp.concatenate(parts, axis=0).astype(bf16)


def d_attn_kernel(d_ref, weight_ref, out_ref):
    product = jnp.dot(d_ref[...], weight_ref[...], preferred_element_type=f32)
    out_ref[...] = product.astype(bf16)


def total_kernel(pieces_ref, out_ref):
    total = jnp.sum(pieces_ref[...].astype(f32), axis=0)
    size = out_ref.shape[0]
    for c in range(out_ref.shape[1] // BLK):
        out_ref[:, c * BLK : (c + 1) * BLK] = total[c * size : (c + 1) * size, :]


def shape(dims, dtype):
    return jax.ShapeDtypeStruct(dims, dtype)


def body(attn, weight, d_out):
    count, width = attn.shape
    features = weight.shape[0]
    group, near, far = lax.axis_size(TENSOR), lax.axis_size(NEAR), lax.axis_size(FAR)
    tall = lax.axis_size("yh")
    rows = count // group
    yh, core = lax.axis_index("yh"), lax.axis_index("core")
    odd = lax.rem(lax.axis_index("x"), 2)

    full_grad = lax.all_gather(d_out, TENSOR, axis=0, tiled=True)
    (packed,) = call(pack_kernel, (shape((near, 2 * count, width), bf16),), (), attn, full_grad)
    packed, attn, full_grad, weight, odd, yh, core = lax.optimization_barrier(
        (packed, attn, full_grad, weight, odd, yh, core)
    )
    pieces = lax.all_to_all(packed, NEAR, 0, 0)
    pieces, attn, full_grad, weight, odd, yh, core = lax.optimization_barrier(
        (pieces, attn, full_grad, weight, odd, yh, core)
    )
    (plane,) = call(
        grad_kernel,
        (shape((far, features // near // far * width // BLK, BLK), bf16),),
        (odd,),
        pieces,
        flops=2 * near * count * WINDOW * width,
    )
    plane, attn, full_grad, core = lax.optimization_barrier((plane, attn, full_grad, core))
    terms = lax.all_to_all(plane, FAR, 0, 0)

    half = shape((tall, rows, features), bf16)
    keep, send = call(
        values_kernel, (half, half), (core,), attn, weight, flops=2 * count * features * (width + 3 * BLK)
    )
    arrived = lax.ppermute(send, "core", [(0, 1), (1, 0)])
    one = shape((rows, features), bf16)
    own, *sent = call(pair_kernel, (shape((rows, features), f32), one, one, one), (yh,), keep, arrived)
    blocks = []
    for step in range(1, tall):
        blocks.append(lax.ppermute(sent[step - 1], "yh", [(i, (i + step) % tall) for i in range(tall)]))
    (d_attn,) = call(
        d_attn_kernel, (shape((count, width), bf16),), (), full_grad, weight, flops=2 * count * features * width
    )
    (mixed,) = call(mixed_kernel, (one,), (), own, *blocks)
    (w_grad,) = call(total_kernel, (shape((features // near // far, width), f32),), (), terms)
    return (mixed, d_attn, w_grad)


def solution(mesh):
    fine = Mesh(mesh.devices.reshape(2, 4, 16, 4, 2), ("yl", "x", "z", "yh", "core"))
    dp = ("yl", "x", "z")
    in_specs = (P(dp, TENSOR), P(None, TENSOR), P(dp + TENSOR, None))
    out_specs = (P(dp + TENSOR, None), P(dp, TENSOR), P(dp, TENSOR))
    return jax.shard_map(body, mesh=fine, in_specs=in_specs, out_specs=out_specs, check_vma=False)
```

```python
import jax
import jax.numpy as jnp
from jax import lax
from jax.experimental import pallas as pl
from jax.experimental.pallas import tpu as pltpu
from jax.sharding import Mesh
from jax.sharding import PartitionSpec as P

BLK = 128
TENSOR = ("yh", "core")
NEAR = ("yl", "x")
FAR = "z"
CHUNKS = 8
WINDOW = 384
VMEM_LIMIT = 16 * 1024 * 1024

code_offset = 6.0
bf16, f32 = jnp.bfloat16, jnp.float32


def call(kernel, outs, scalars, *arrays, flops=0):
    specs = [pl.BlockSpec(memory_space=pltpu.SMEM)] * len(scalars)
    specs += [pl.BlockSpec(memory_space=pltpu.VMEM)] * len(arrays)
    moved = sum(a.size * a.dtype.itemsize for a in tuple(arrays) + tuple(outs))
    return pl.pallas_call(
        kernel,
        out_shape=outs,
        in_specs=specs,
        out_specs=tuple(pl.BlockSpec(memory_space=pltpu.VMEM) for _ in outs),
        compiler_params=pltpu.CompilerParams(vmem_limit_bytes=VMEM_LIMIT),
        cost_estimate=pl.CostEstimate(flops=flops, bytes_accessed=moved, transcendentals=0),
    )(*[jnp.reshape(s, (1,)).astype(jnp.int32) for s in scalars], *arrays)


def signs_table():
    rows = lax.broadcasted_iota(jnp.int32, (BLK, BLK), 0)
    cols = lax.broadcasted_iota(jnp.int32, (BLK, BLK), 1)
    common = jnp.bitwise_and(rows, cols)
    parity = jnp.zeros((BLK, BLK), jnp.int32)
    for place in range(BLK.bit_length() - 1):
        parity = parity + jnp.bitwise_and(jnp.right_shift(common, place), 1)
    return (1 - 2 * jnp.bitwise_and(parity, 1)).astype(f32).astype(bf16)


def rotate(field, table):
    high = field.astype(bf16)
    rest = field - high.astype(f32)
    middle = rest.astype(bf16)
    low = (rest - middle.astype(f32)).astype(bf16)
    turned = jnp.dot(high, table, preferred_element_type=f32)
    turned += jnp.dot(middle, table, preferred_element_type=f32)
    turned += jnp.dot(low, table, preferred_element_type=f32)
    return turned * (BLK**-0.5)


def pack_kernel(attn_ref, d_ref, out_ref, attn_here, d_here, sems):
    count, rows = attn_here.shape[0], d_here.shape[0]
    first = pltpu.make_async_copy(attn_ref, attn_here, sems.at[0])
    second = pltpu.make_async_copy(d_ref, d_here, sems.at[1])
    first.start()
    second.start()
    copies = []
    for i in range(CHUNKS):
        copies.append((attn_here, out_ref.at[i, pl.ds(0, count), :]))
    for i in range(CHUNKS):
        window = d_here.at[:, pl.ds(i * 320 // BLK * BLK, WINDOW)]
        copies.append((window, out_ref.at[i, pl.ds(count, rows), :]))
    copies = [pltpu.make_async_copy(a, b, sems.at[2 + k]) for k, (a, b) in enumerate(copies)]
    first.wait()
    for copy in copies[:CHUNKS]:
        copy.start()
    second.wait()
    for copy in copies[CHUNKS:]:
        copy.start()
    for copy in copies:
        copy.wait()


def pack(attn, d_out):
    out = shape((CHUNKS, attn.shape[0] + d_out.shape[0], attn.shape[1]), bf16)
    return pl.pallas_call(
        pack_kernel,
        out_shape=out,
        in_specs=[pl.BlockSpec(memory_space=pltpu.HBM)] * 2,
        out_specs=pl.BlockSpec(memory_space=pltpu.HBM),
        scratch_shapes=[
            pltpu.VMEM(attn.shape, bf16),
            pltpu.VMEM(d_out.shape, bf16),
            pltpu.SemaphoreType.DMA((2 + 2 * CHUNKS,)),
        ],
        compiler_params=pltpu.CompilerParams(vmem_limit_bytes=VMEM_LIMIT),
        cost_estimate=pl.CostEstimate(flops=0, bytes_accessed=3 * out.size, transcendentals=0),
    )(attn, d_out)


def values_kernel(core_ref, attn_ref, weight_ref, keep_ref, send_ref):
    table = signs_table()
    count, features = attn_ref.shape[0], weight_ref.shape[0]
    tall, rows = keep_ref.shape[0], keep_ref.shape[1]
    first = core_ref[0] == 0
    for j in range(features // BLK):
        cols = slice(j * BLK, (j + 1) * BLK)
        partial_value = lax.dot_general(
            attn_ref[...], weight_ref[cols, :], (((1,), (1,)), ((), ())), preferred_element_type=f32
        )
        turned = rotate(partial_value, table)
        top = jnp.max(jnp.abs(turned), axis=1, keepdims=True) + 1e-06
        scale = top.astype(bf16).astype(f32)
        coded = (turned / scale + code_offset).astype(bf16)
        values = ((coded.astype(f32) - code_offset) * scale).reshape(tall, 2, rows, BLK)
        zero, one = values[:, 0], values[:, 1]
        keep_ref[:, :, cols] = jnp.where(first, zero, one).astype(bf16)
        send_ref[:, :, cols] = jnp.where(first, one, zero).astype(bf16)


def pair_kernel(me_ref, keep_ref, arrived_ref, d_ref, own_ref, *sent_refs):
    tall, rows = keep_ref.shape[:2]
    me = me_ref[0]
    own_ref[...] = keep_ref[me].astype(f32) + arrived_ref[me].astype(f32)
    for step in range(1, tall):
        other = lax.rem(me + step, tall)
        total = keep_ref[other].astype(f32) + arrived_ref[other].astype(f32)
        sent_refs[step - 1][:rows, :] = total.astype(bf16)
        sent_refs[step - 1][rows:, :] = d_ref[...]


def mixed_kernel(me_ref, own_ref, d_ref, a_ref, b_ref, c_ref, out_ref, half_ref):
    table = signs_table()
    tall, rows = half_ref.shape[:2]
    me = me_ref[0]
    half_ref[me] = d_ref[...]
    for step, ref in ((1, a_ref), (2, b_ref), (3, c_ref)):
        half_ref[lax.rem(me + tall - step, tall)] = ref[rows:, :]
    for j in range(out_ref.shape[1] // BLK):
        cols = slice(j * BLK, (j + 1) * BLK)
        total = own_ref[:, cols] + a_ref[:rows, cols].astype(f32)
        total += b_ref[:rows, cols].astype(f32) + c_ref[:rows, cols].astype(f32)
        out_ref[:, cols] = rotate(total, table).astype(bf16)


def grad_kernel(odd_ref, near_ref, d_ref, out_ref):
    near, group, rows = d_ref.shape[1], d_ref.shape[0], d_ref.shape[2]
    count = group * rows
    left = jnp.concatenate([d_ref[:, p].reshape(count, WINDOW) for p in range(near)], axis=0)
    right = jnp.concatenate([near_ref[p, :count, :] for p in range(near)], axis=0)
    term = lax.dot_general(left, right, (((0,), (0,)), ((), ())), preferred_element_type=f32)
    far, size = out_ref.shape[0], out_ref.shape[1] * BLK // term.shape[1]
    chunk = far * size
    term = jnp.where(odd_ref[0] == 1, term[WINDOW - chunk :, :], term[:chunk, :])
    for z in range(far):
        block = term[z * size : (z + 1) * size, :]
        parts = [block[:, c : c + BLK] for c in range(0, term.shape[1], BLK)]
        out_ref[z] = jnp.concatenate(parts, axis=0).astype(bf16)


def d_attn_kernel(core_ref, half_ref, other_ref, weight_ref, out_ref):
    tall, _, rows, width = out_ref.shape
    first = core_ref[0] == 0
    mine, theirs = half_ref[...], other_ref[...]
    zero = jnp.where(first, mine, theirs).reshape(tall * rows, -1)
    one = jnp.where(first, theirs, mine).reshape(tall * rows, -1)
    both = jnp.concatenate([zero, one], axis=0)
    product = jnp.dot(both, weight_ref[...], preferred_element_type=f32).astype(bf16)
    out_ref[:, 0] = product[: tall * rows].reshape(tall, rows, width)
    out_ref[:, 1] = product[tall * rows :].reshape(tall, rows, width)


def total_kernel(pieces_ref, out_ref):
    total = jnp.sum(pieces_ref[...].astype(f32), axis=0)
    size = out_ref.shape[0]
    for c in range(out_ref.shape[1] // BLK):
        out_ref[:, c * BLK : (c + 1) * BLK] = total[c * size : (c + 1) * size, :]


def shape(dims, dtype):
    return jax.ShapeDtypeStruct(dims, dtype)


def body(attn, weight, d_out):
    count, width = attn.shape
    features = weight.shape[0]
    group, near, far = lax.axis_size(TENSOR), lax.axis_size(NEAR), lax.axis_size(FAR)
    tall = lax.axis_size("yh")
    rows = count // group
    yh, core = lax.axis_index("yh"), lax.axis_index("core")
    odd = lax.rem(lax.axis_index("x"), 2)

    packed = pack(attn, d_out)
    packed, attn = lax.optimization_barrier((packed, attn))
    pieces = lax.all_to_all(packed, NEAR, 0, 0)

    half = shape((tall, rows, features), bf16)
    keep, send = call(
        values_kernel, (half, half), (core,), attn, weight, flops=2 * count * features * (width + 3 * BLK)
    )
    arrived = lax.ppermute(send, "core", [(0, 1), (1, 0)])
    one, two = shape((rows, features), bf16), shape((2 * rows, features), bf16)
    own, *sent = call(
        pair_kernel, (shape((rows, features), f32), two, two, two), (yh,), keep, arrived, d_out
    )
    rings = [[(i, (i + step) % tall) for i in range(tall)] for step in range(tall)]
    first = lax.ppermute(sent[0], "yh", rings[1])

    pieces, first, sent = lax.optimization_barrier((pieces, first, sent))
    chunk = lax.all_gather(pieces[:, count:, :], TENSOR)
    (plane,) = call(
        grad_kernel,
        (shape((far, features // near // far * width // BLK, BLK), bf16),),
        (odd,),
        pieces,
        chunk,
        flops=2 * near * count * WINDOW * width,
    )
    plane, sent = lax.optimization_barrier((plane, sent))
    terms = lax.all_to_all(plane, FAR, 0, 0)

    blocks = [first] + [lax.ppermute(sent[step - 1], "yh", rings[step]) for step in range(2, tall)]
    mixed, mine = call(mixed_kernel, (one, half), (yh,), own, d_out, *blocks)
    theirs = lax.ppermute(mine, "core", [(0, 1), (1, 0)])
    (d_attn,) = call(
        d_attn_kernel,
        (shape((tall, group // tall, rows, width), bf16),),
        (core,),
        mine,
        theirs,
        weight,
        flops=2 * count * features * width,
    )
    d_attn = d_attn.reshape(count, width)
    (w_grad,) = call(total_kernel, (shape((features // near // far, width), f32),), (), terms)
    return (mixed, d_attn, w_grad)


def solution(mesh):
    fine = Mesh(mesh.devices.reshape(2, 4, 16, 4, 2), ("yl", "x", "z", "yh", "core"))
    dp = ("yl", "x", "z")
    in_specs = (P(dp, TENSOR), P(None, TENSOR), P(dp + TENSOR, None))
    out_specs = (P(dp + TENSOR, None), P(dp, TENSOR), P(dp, TENSOR))
    return jax.shard_map(body, mesh=fine, in_specs=in_specs, out_specs=out_specs, check_vma=False)
```

```python
import jax
import jax.numpy as jnp
from jax import lax
from jax.experimental import pallas as pl
from jax.experimental.pallas import tpu as pltpu
from jax.sharding import Mesh
from jax.sharding import PartitionSpec as P

BLK = 128
TENSOR = ("yh", "core")
NEAR = ("yl", "x")
FAR = "z"
CHUNKS = 8
WINDOW = 384
VMEM_LIMIT = 16 * 1024 * 1024

code_offset = 6.0
bf16, f32 = jnp.bfloat16, jnp.float32


def call(kernel, outs, scalars, *arrays, flops=0):
    specs = [pl.BlockSpec(memory_space=pltpu.SMEM)] * len(scalars)
    specs += [pl.BlockSpec(memory_space=pltpu.VMEM)] * len(arrays)
    moved = sum(a.size * a.dtype.itemsize for a in tuple(arrays) + tuple(outs))
    return pl.pallas_call(
        kernel,
        out_shape=outs,
        in_specs=specs,
        out_specs=tuple(pl.BlockSpec(memory_space=pltpu.VMEM) for _ in outs),
        compiler_params=pltpu.CompilerParams(vmem_limit_bytes=VMEM_LIMIT),
        cost_estimate=pl.CostEstimate(flops=flops, bytes_accessed=moved, transcendentals=0),
    )(*[jnp.reshape(s, (1,)).astype(jnp.int32) for s in scalars], *arrays)


def signs_table():
    rows = lax.broadcasted_iota(jnp.int32, (BLK, BLK), 0)
    cols = lax.broadcasted_iota(jnp.int32, (BLK, BLK), 1)
    common = jnp.bitwise_and(rows, cols)
    parity = jnp.zeros((BLK, BLK), jnp.int32)
    for place in range(BLK.bit_length() - 1):
        parity = parity + jnp.bitwise_and(jnp.right_shift(common, place), 1)
    return (1 - 2 * jnp.bitwise_and(parity, 1)).astype(f32).astype(bf16)


def rotate(field, table):
    high = field.astype(bf16)
    rest = field - high.astype(f32)
    middle = rest.astype(bf16)
    low = (rest - middle.astype(f32)).astype(bf16)
    turned = jnp.dot(high, table, preferred_element_type=f32)
    turned += jnp.dot(middle, table, preferred_element_type=f32)
    turned += jnp.dot(low, table, preferred_element_type=f32)
    return turned * (BLK**-0.5)


def pack_kernel(attn_ref, d_ref, out_ref):
    count = attn_ref.shape[0]
    for i in range(CHUNKS):
        start = i * 320 // BLK * BLK
        out_ref[i, :count, :] = attn_ref[...]
        out_ref[i, count:, :] = d_ref[:, start : start + WINDOW]


def values_kernel(core_ref, attn_ref, weight_ref, keep_ref, send_ref):
    table = signs_table()
    count, features = attn_ref.shape[0], weight_ref.shape[0]
    tall, rows = keep_ref.shape[0], keep_ref.shape[1]
    first = core_ref[0] == 0
    for j in range(features // BLK):
        cols = slice(j * BLK, (j + 1) * BLK)
        partial_value = lax.dot_general(
            attn_ref[...], weight_ref[cols, :], (((1,), (1,)), ((), ())), preferred_element_type=f32
        )
        turned = rotate(partial_value, table)
        top = jnp.max(jnp.abs(turned), axis=1, keepdims=True) + 1e-06
        scale = top.astype(bf16).astype(f32)
        coded = (turned / scale + code_offset).astype(bf16)
        values = ((coded.astype(f32) - code_offset) * scale).reshape(tall, 2, rows, BLK)
        zero, one = values[:, 0], values[:, 1]
        keep_ref[:, :, cols] = jnp.where(first, zero, one).astype(bf16)
        send_ref[:, :, cols] = jnp.where(first, one, zero).astype(bf16)


def pair_kernel(me_ref, keep_ref, arrived_ref, own_ref, *sent_refs):
    tall = keep_ref.shape[0]
    me = me_ref[0]
    own_ref[...] = keep_ref[me].astype(f32) + arrived_ref[me].astype(f32)
    for step in range(1, tall):
        other = lax.rem(me + step, tall)
        total = keep_ref[other].astype(f32) + arrived_ref[other].astype(f32)
        sent_refs[step - 1][...] = total.astype(bf16)


def mixed_kernel(own_ref, a_ref, b_ref, c_ref, out_ref):
    table = signs_table()
    for j in range(out_ref.shape[1] // BLK):
        cols = slice(j * BLK, (j + 1) * BLK)
        total = own_ref[:, cols] + a_ref[:, cols].astype(f32)
        total += b_ref[:, cols].astype(f32) + c_ref[:, cols].astype(f32)
        out_ref[:, cols] = rotate(total, table).astype(bf16)


def grad_kernel(odd_ref, near_ref, out_ref):
    near, count = near_ref.shape[0], near_ref.shape[1] // 2
    left = jnp.concatenate([near_ref[p, count:, :] for p in range(near)], axis=0)
    right = jnp.concatenate([near_ref[p, :count, :] for p in range(near)], axis=0)
    term = lax.dot_general(left, right, (((0,), (0,)), ((), ())), preferred_element_type=f32)
    far, size = out_ref.shape[0], out_ref.shape[1] * BLK // term.shape[1]
    chunk = far * size
    term = jnp.where(odd_ref[0] == 1, term[WINDOW - chunk :, :], term[:chunk, :])
    for z in range(far):
        block = term[z * size : (z + 1) * size, :]
        parts = [block[:, c : c + BLK] for c in range(0, term.shape[1], BLK)]
        out_ref[z] = jnp.concatenate(parts, axis=0).astype(bf16)


def d_attn_kernel(d_ref, weight_ref, out_ref):
    product = jnp.dot(d_ref[...], weight_ref[...], preferred_element_type=f32)
    out_ref[...] = product.astype(bf16)


def total_kernel(pieces_ref, out_ref):
    total = jnp.sum(pieces_ref[...].astype(f32), axis=0)
    size = out_ref.shape[0]
    for c in range(out_ref.shape[1] // BLK):
        out_ref[:, c * BLK : (c + 1) * BLK] = total[c * size : (c + 1) * size, :]


def shape(dims, dtype):
    return jax.ShapeDtypeStruct(dims, dtype)


def body(attn, weight, d_out):
    count, width = attn.shape
    features = weight.shape[0]
    group, near, far = lax.axis_size(TENSOR), lax.axis_size(NEAR), lax.axis_size(FAR)
    tall = lax.axis_size("yh")
    rows = count // group
    yh, core = lax.axis_index("yh"), lax.axis_index("core")
    odd = lax.rem(lax.axis_index("x"), 2)

    full_grad = lax.all_gather(d_out, TENSOR, axis=0, tiled=True)
    (packed,) = call(pack_kernel, (shape((near, 2 * count, width), bf16),), (), attn, full_grad)
    packed, attn = lax.optimization_barrier((packed, attn))
    pieces = lax.all_to_all(packed, NEAR, 0, 0)

    (d_attn,) = call(
        d_attn_kernel, (shape((count, width), bf16),), (), full_grad, weight, flops=2 * count * features * width
    )
    attn, d_attn = lax.optimization_barrier((attn, d_attn))
    half = shape((tall, rows, features), bf16)
    keep, send = call(
        values_kernel, (half, half), (core,), attn, weight, flops=2 * count * features * (width + 3 * BLK)
    )
    arrived = lax.ppermute(send, "core", [(0, 1), (1, 0)])
    one = shape((rows, features), bf16)
    own, *sent = call(pair_kernel, (shape((rows, features), f32), one, one, one), (yh,), keep, arrived)

    pieces, sent, d_attn = lax.optimization_barrier((pieces, sent, d_attn))
    (plane,) = call(
        grad_kernel,
        (shape((far, features // near // far * width // BLK, BLK), bf16),),
        (odd,),
        pieces,
        flops=2 * near * count * WINDOW * width,
    )
    plane, sent = lax.optimization_barrier((plane, sent))
    terms = lax.all_to_all(plane, FAR, 0, 0)

    blocks = []
    for step in range(1, tall):
        blocks.append(lax.ppermute(sent[step - 1], "yh", [(i, (i + step) % tall) for i in range(tall)]))
    (mixed,) = call(mixed_kernel, (one,), (), own, *blocks)
    (w_grad,) = call(total_kernel, (shape((features // near // far, width), f32),), (), terms)
    return (mixed, d_attn, w_grad)


def solution(mesh):
    fine = Mesh(mesh.devices.reshape(2, 4, 16, 4, 2), ("yl", "x", "z", "yh", "core"))
    dp = ("yl", "x", "z")
    in_specs = (P(dp, TENSOR), P(None, TENSOR), P(dp + TENSOR, None))
    out_specs = (P(dp + TENSOR, None), P(dp, TENSOR), P(dp, TENSOR))
    return jax.shard_map(body, mesh=fine, in_specs=in_specs, out_specs=out_specs, check_vma=False)
```

```python
import jax
import jax.numpy as jnp
from jax import lax
from jax.experimental import pallas as pl
from jax.experimental.pallas import tpu as pltpu
from jax.sharding import Mesh
from jax.sharding import PartitionSpec as P

BLK = 128
TENSOR = ("yh", "core")
NEAR = ("yl", "x")
FAR = "z"
CHUNKS = 8
WINDOW = 384
VMEM_LIMIT = 16 * 1024 * 1024

code_offset = 6.0
bf16, f32 = jnp.bfloat16, jnp.float32


def call(kernel, outs, scalars, *arrays, flops=0):
    specs = [pl.BlockSpec(memory_space=pltpu.SMEM)] * len(scalars)
    specs += [pl.BlockSpec(memory_space=pltpu.VMEM)] * len(arrays)
    moved = sum(a.size * a.dtype.itemsize for a in tuple(arrays) + tuple(outs))
    return pl.pallas_call(
        kernel,
        out_shape=outs,
        in_specs=specs,
        out_specs=tuple(pl.BlockSpec(memory_space=pltpu.VMEM) for _ in outs),
        compiler_params=pltpu.CompilerParams(vmem_limit_bytes=VMEM_LIMIT),
        cost_estimate=pl.CostEstimate(flops=flops, bytes_accessed=moved, transcendentals=0),
    )(*[jnp.reshape(s, (1,)).astype(jnp.int32) for s in scalars], *arrays)


def signs_table():
    rows = lax.broadcasted_iota(jnp.int32, (BLK, BLK), 0)
    cols = lax.broadcasted_iota(jnp.int32, (BLK, BLK), 1)
    common = jnp.bitwise_and(rows, cols)
    parity = jnp.zeros((BLK, BLK), jnp.int32)
    for place in range(BLK.bit_length() - 1):
        parity = parity + jnp.bitwise_and(jnp.right_shift(common, place), 1)
    return (1 - 2 * jnp.bitwise_and(parity, 1)).astype(f32).astype(bf16)


def rotate(field, table):
    high = field.astype(bf16)
    rest = field - high.astype(f32)
    middle = rest.astype(bf16)
    low = (rest - middle.astype(f32)).astype(bf16)
    turned = jnp.dot(high, table, preferred_element_type=f32)
    turned += jnp.dot(middle, table, preferred_element_type=f32)
    turned += jnp.dot(low, table, preferred_element_type=f32)
    return turned * (BLK**-0.5)


def pack_kernel(attn_ref, d_ref, out_ref, attn_here, d_here, sems):
    count = attn_here.shape[0]
    first = pltpu.make_async_copy(attn_ref, attn_here, sems.at[0])
    second = pltpu.make_async_copy(d_ref, d_here, sems.at[1])
    first.start()
    second.start()
    copies = []
    for i in range(CHUNKS):
        copies.append((attn_here, out_ref.at[i, pl.ds(0, count), :]))
    for i in range(CHUNKS):
        window = d_here.at[:, pl.ds(i * 320 // BLK * BLK, WINDOW)]
        copies.append((window, out_ref.at[i, pl.ds(count, count), :]))
    copies = [pltpu.make_async_copy(a, b, sems.at[2 + k]) for k, (a, b) in enumerate(copies)]
    first.wait()
    for copy in copies[:CHUNKS]:
        copy.start()
    second.wait()
    for copy in copies[CHUNKS:]:
        copy.start()
    for copy in copies:
        copy.wait()


def pack(attn, full_grad):
    out = shape((CHUNKS, 2 * attn.shape[0], attn.shape[1]), bf16)
    return pl.pallas_call(
        pack_kernel,
        out_shape=out,
        in_specs=[pl.BlockSpec(memory_space=pltpu.HBM)] * 2,
        out_specs=pl.BlockSpec(memory_space=pltpu.HBM),
        scratch_shapes=[
            pltpu.VMEM(attn.shape, bf16),
            pltpu.VMEM(full_grad.shape, bf16),
            pltpu.SemaphoreType.DMA((2 + 2 * CHUNKS,)),
        ],
        cost_estimate=pl.CostEstimate(flops=0, bytes_accessed=3 * out.size, transcendentals=0),
    )(attn, full_grad)


def values_kernel(core_ref, attn_ref, weight_ref, keep_ref, send_ref):
    table = signs_table()
    count, features = attn_ref.shape[0], weight_ref.shape[0]
    tall, rows = keep_ref.shape[0], keep_ref.shape[1]
    first = core_ref[0] == 0
    for j in range(features // BLK):
        cols = slice(j * BLK, (j + 1) * BLK)
        partial_value = lax.dot_general(
            attn_ref[...], weight_ref[cols, :], (((1,), (1,)), ((), ())), preferred_element_type=f32
        )
        turned = rotate(partial_value, table)
        top = jnp.max(jnp.abs(turned), axis=1, keepdims=True) + 1e-06
        scale = top.astype(bf16).astype(f32)
        coded = (turned / scale + code_offset).astype(bf16)
        values = ((coded.astype(f32) - code_offset) * scale).reshape(tall, 2, rows, BLK)
        zero, one = values[:, 0], values[:, 1]
        keep_ref[:, :, cols] = jnp.where(first, zero, one).astype(bf16)
        send_ref[:, :, cols] = jnp.where(first, one, zero).astype(bf16)


def pair_kernel(me_ref, keep_ref, arrived_ref, own_ref, *sent_refs):
    tall = keep_ref.shape[0]
    me = me_ref[0]
    own_ref[...] = keep_ref[me].astype(f32) + arrived_ref[me].astype(f32)
    for step in range(1, tall):
        other = lax.rem(me + step, tall)
        total = keep_ref[other].astype(f32) + arrived_ref[other].astype(f32)
        sent_refs[step - 1][...] = total.astype(bf16)


def mixed_kernel(own_ref, a_ref, b_ref, c_ref, out_ref):
    table = signs_table()
    for j in range(out_ref.shape[1] // BLK):
        cols = slice(j * BLK, (j + 1) * BLK)
        total = own_ref[:, cols] + a_ref[:, cols].astype(f32)
        total += b_ref[:, cols].astype(f32) + c_ref[:, cols].astype(f32)
        out_ref[:, cols] = rotate(total, table).astype(bf16)


def grad_kernel(odd_ref, near_ref, out_ref):
    near, count = near_ref.shape[0], near_ref.shape[1] // 2
    left = jnp.concatenate([near_ref[p, count:, :] for p in range(near)], axis=0)
    right = jnp.concatenate([near_ref[p, :count, :] for p in range(near)], axis=0)
    term = lax.dot_general(left, right, (((0,), (0,)), ((), ())), preferred_element_type=f32)
    far, size = out_ref.shape[0], out_ref.shape[1] * BLK // term.shape[1]
    chunk = far * size
    term = jnp.where(odd_ref[0] == 1, term[WINDOW - chunk :, :], term[:chunk, :])
    for z in range(far):
        block = term[z * size : (z + 1) * size, :]
        parts = [block[:, c : c + BLK] for c in range(0, term.shape[1], BLK)]
        out_ref[z] = jnp.concatenate(parts, axis=0).astype(bf16)


def d_attn_kernel(d_ref, weight_ref, out_ref):
    product = jnp.dot(d_ref[...], weight_ref[...], preferred_element_type=f32)
    out_ref[...] = product.astype(bf16)


def total_kernel(pieces_ref, out_ref):
    total = jnp.sum(pieces_ref[...].astype(f32), axis=0)
    size = out_ref.shape[0]
    for c in range(out_ref.shape[1] // BLK):
        out_ref[:, c * BLK : (c + 1) * BLK] = total[c * size : (c + 1) * size, :]


def shape(dims, dtype):
    return jax.ShapeDtypeStruct(dims, dtype)


def body(attn, weight, d_out):
    count, width = attn.shape
    features = weight.shape[0]
    group, near, far = lax.axis_size(TENSOR), lax.axis_size(NEAR), lax.axis_size(FAR)
    tall = lax.axis_size("yh")
    rows = count // group
    yh, core = lax.axis_index("yh"), lax.axis_index("core")
    odd = lax.rem(lax.axis_index("x"), 2)

    full_grad = lax.all_gather(d_out, TENSOR, axis=0, tiled=True)
    packed = pack(attn, full_grad)
    packed, attn = lax.optimization_barrier((packed, attn))
    pieces = lax.all_to_all(packed, NEAR, 0, 0)

    (d_attn,) = call(
        d_attn_kernel, (shape((count, width), bf16),), (), full_grad, weight, flops=2 * count * features * width
    )
    attn, d_attn = lax.optimization_barrier((attn, d_attn))
    half = shape((tall, rows, features), bf16)
    keep, send = call(
        values_kernel, (half, half), (core,), attn, weight, flops=2 * count * features * (width + 3 * BLK)
    )
    arrived = lax.ppermute(send, "core", [(0, 1), (1, 0)])
    one = shape((rows, features), bf16)
    own, *sent = call(pair_kernel, (shape((rows, features), f32), one, one, one), (yh,), keep, arrived)

    pieces, sent, d_attn = lax.optimization_barrier((pieces, sent, d_attn))
    (plane,) = call(
        grad_kernel,
        (shape((far, features // near // far * width // BLK, BLK), bf16),),
        (odd,),
        pieces,
        flops=2 * near * count * WINDOW * width,
    )
    plane, sent = lax.optimization_barrier((plane, sent))
    terms = lax.all_to_all(plane, FAR, 0, 0)

    blocks = []
    for step in range(1, tall):
        blocks.append(lax.ppermute(sent[step - 1], "yh", [(i, (i + step) % tall) for i in range(tall)]))
    (mixed,) = call(mixed_kernel, (one,), (), own, *blocks)
    (w_grad,) = call(total_kernel, (shape((features // near // far, width), f32),), (), terms)
    return (mixed, d_attn, w_grad)


def solution(mesh):
    fine = Mesh(mesh.devices.reshape(2, 4, 16, 4, 2), ("yl", "x", "z", "yh", "core"))
    dp = ("yl", "x", "z")
    in_specs = (P(dp, TENSOR), P(None, TENSOR), P(dp + TENSOR, None))
    out_specs = (P(dp + TENSOR, None), P(dp, TENSOR), P(dp, TENSOR))
    return jax.shard_map(body, mesh=fine, in_specs=in_specs, out_specs=out_specs, check_vma=False)
```

```python
import jax
import jax.numpy as jnp
from jax import lax
from jax.experimental import pallas as pl
from jax.experimental.pallas import tpu as pltpu
from jax.sharding import Mesh
from jax.sharding import PartitionSpec as P

BLK = 128
TENSOR = ("yh", "core")
NEAR = ("yl", "x")
FAR = "z"
CHUNKS = 8
WINDOW = 384
VMEM_LIMIT = 16 * 1024 * 1024

code_offset = 6.0
bf16, f32 = jnp.bfloat16, jnp.float32


def call(kernel, outs, scalars, *arrays, flops=0):
    specs = [pl.BlockSpec(memory_space=pltpu.SMEM)] * len(scalars)
    specs += [pl.BlockSpec(memory_space=pltpu.VMEM)] * len(arrays)
    moved = sum(a.size * a.dtype.itemsize for a in tuple(arrays) + tuple(outs))
    return pl.pallas_call(
        kernel,
        out_shape=outs,
        in_specs=specs,
        out_specs=tuple(pl.BlockSpec(memory_space=pltpu.VMEM) for _ in outs),
        compiler_params=pltpu.CompilerParams(vmem_limit_bytes=VMEM_LIMIT),
        cost_estimate=pl.CostEstimate(flops=flops, bytes_accessed=moved, transcendentals=0),
    )(*[jnp.reshape(s, (1,)).astype(jnp.int32) for s in scalars], *arrays)


def signs_table():
    rows = lax.broadcasted_iota(jnp.int32, (BLK, BLK), 0)
    cols = lax.broadcasted_iota(jnp.int32, (BLK, BLK), 1)
    common = jnp.bitwise_and(rows, cols)
    parity = jnp.zeros((BLK, BLK), jnp.int32)
    for place in range(BLK.bit_length() - 1):
        parity = parity + jnp.bitwise_and(jnp.right_shift(common, place), 1)
    return (1 - 2 * jnp.bitwise_and(parity, 1)).astype(f32).astype(bf16)


def rotate(field, table):
    high = field.astype(bf16)
    rest = field - high.astype(f32)
    middle = rest.astype(bf16)
    low = (rest - middle.astype(f32)).astype(bf16)
    turned = jnp.dot(high, table, preferred_element_type=f32)
    turned += jnp.dot(middle, table, preferred_element_type=f32)
    turned += jnp.dot(low, table, preferred_element_type=f32)
    return turned * (BLK**-0.5)


def pack_kernel(attn_ref, d_ref, out_ref, grads_ref, attn_here, d_here, stage_a, stage_d, sems):
    count, width = attn_here.shape
    half = count // 2
    first = pltpu.make_async_copy(attn_ref, attn_here, sems.at[0])
    second = pltpu.make_async_copy(d_ref, d_here, sems.at[1])
    first.start()
    second.start()
    copies = []

    def send(source, target):
        copies.append(pltpu.make_async_copy(source, target, sems.at[2 + len(copies)]))
        copies[-1].start()

    first.wait()
    for c in range(width // BLK):
        stage_a[c * count : (c + 1) * count, :] = attn_here[:, c * BLK : (c + 1) * BLK]
    for i in range(CHUNKS):
        send(stage_a, out_ref.at[i, pl.ds(0, stage_a.shape[0]), :])
    second.wait()
    send(d_here, grads_ref)
    low = lax.broadcasted_iota(jnp.int32, (half, BLK), 1) < BLK // 2
    for i in range(CHUNKS):
        pair = i // 2 * 5 * BLK
        for k in range(2):
            start = pair + (3 * BLK if i % 2 else 0) + k * BLK
            stage_d[i, k * count : (k + 1) * count, :] = d_here[:, start : start + BLK]
        tile = d_here[:, pair + 2 * BLK : pair + 3 * BLK].astype(f32)
        top, bottom = tile[:half], tile[half:]
        if i % 2:
            fold = jnp.where(low, pltpu.roll(top, BLK // 2, 1), bottom)
        else:
            fold = jnp.where(low, top, pltpu.roll(bottom, BLK // 2, 1))
        stage_d[i, 2 * count :, :] = fold.astype(bf16)
        send(stage_d.at[i], out_ref.at[i, pl.ds(stage_a.shape[0], stage_d.shape[1]), :])
    for copy in copies:
        copy.wait()


def pack(attn, full_grad):
    (count, width), features = attn.shape, full_grad.shape[1]
    lines = (count * width // BLK, count * features // CHUNKS // BLK)
    return pl.pallas_call(
        pack_kernel,
        out_shape=(shape((CHUNKS, sum(lines), BLK), bf16), shape(full_grad.shape, bf16)),
        in_specs=[pl.BlockSpec(memory_space=pltpu.HBM)] * 2,
        out_specs=(pl.BlockSpec(memory_space=pltpu.HBM),) * 2,
        scratch_shapes=[
            pltpu.VMEM(attn.shape, bf16),
            pltpu.VMEM(full_grad.shape, bf16),
            pltpu.VMEM((lines[0], BLK), bf16),
            pltpu.VMEM((CHUNKS, lines[1], BLK), bf16),
            pltpu.SemaphoreType.DMA((3 + 2 * CHUNKS,)),
        ],
        cost_estimate=pl.CostEstimate(flops=0, bytes_accessed=10**7, transcendentals=0),
    )(attn, full_grad)


def values_kernel(core_ref, attn_ref, weight_ref, keep_ref, send_ref):
    table = signs_table()
    count, features = attn_ref.shape[0], weight_ref.shape[0]
    tall, rows = keep_ref.shape[0], keep_ref.shape[1]
    first = core_ref[0] == 0
    for j in range(features // BLK):
        cols = slice(j * BLK, (j + 1) * BLK)
        partial_value = lax.dot_general(
            attn_ref[...], weight_ref[cols, :], (((1,), (1,)), ((), ())), preferred_element_type=f32
        )
        turned = rotate(partial_value, table)
        top = jnp.max(jnp.abs(turned), axis=1, keepdims=True) + 1e-06
        scale = top.astype(bf16).astype(f32)
        coded = (turned / scale + code_offset).astype(bf16)
        values = ((coded.astype(f32) - code_offset) * scale).reshape(tall, 2, rows, BLK)
        zero, one = values[:, 0], values[:, 1]
        keep_ref[:, :, cols] = jnp.where(first, zero, one).astype(bf16)
        send_ref[:, :, cols] = jnp.where(first, one, zero).astype(bf16)


def pair_kernel(me_ref, keep_ref, arrived_ref, own_ref, *sent_refs):
    tall = keep_ref.shape[0]
    me = me_ref[0]
    own_ref[...] = keep_ref[me].astype(f32) + arrived_ref[me].astype(f32)
    for step in range(1, tall):
        other = lax.rem(me + step, tall)
        total = keep_ref[other].astype(f32) + arrived_ref[other].astype(f32)
        sent_refs[step - 1][...] = total.astype(bf16)


def mixed_kernel(own_ref, a_ref, b_ref, c_ref, out_ref):
    table = signs_table()
    for j in range(out_ref.shape[1] // BLK):
        cols = slice(j * BLK, (j + 1) * BLK)
        total = own_ref[:, cols] + a_ref[:, cols].astype(f32)
        total += b_ref[:, cols].astype(f32) + c_ref[:, cols].astype(f32)
        out_ref[:, cols] = rotate(total, table).astype(bf16)


def grad_kernel(odd_ref, near_ref, out_ref):
    far, size = out_ref.shape[0], out_ref.shape[1] * BLK // WINDOW
    near, count, tiles = near_ref.shape[0], BLK, WINDOW // BLK
    half = count // 2

    def piece(p, k):
        return near_ref[p, k * count : (k + 1) * count, :]

    def times(left, right):
        return lax.dot_general(left, right, (((0,), (0,)), ((), ())), preferred_element_type=f32)

    attns = [jnp.concatenate([piece(p, k) for k in range(tiles)], axis=1) for p in range(near)]
    whole = jnp.concatenate(
        [jnp.concatenate([piece(p, tiles), piece(p, tiles + 1)], axis=1) for p in range(near)], axis=0
    )
    whole = times(whole, jnp.concatenate(attns, axis=0))
    folds = jnp.concatenate([near_ref[p, (tiles + 2) * count :, :] for p in range(near)], axis=0)
    top = times(folds, jnp.concatenate([a[:half] for a in attns], axis=0))
    bottom = times(folds, jnp.concatenate([a[half:] for a in attns], axis=0))
    rest = top[: BLK // 2] + bottom[BLK // 2 :]
    even, odd = jnp.concatenate([whole, rest], axis=0), jnp.concatenate([rest, whole], axis=0)
    term = jnp.where(odd_ref[0] == 1, odd, even)
    for z in range(far):
        block = term[z * size : (z + 1) * size, :]
        parts = [block[:, c : c + BLK] for c in range(0, term.shape[1], BLK)]
        out_ref[z] = jnp.concatenate(parts, axis=0).astype(bf16)


def d_attn_kernel(d_ref, weight_ref, out_ref):
    product = jnp.dot(d_ref[...], weight_ref[...], preferred_element_type=f32)
    out_ref[...] = product.astype(bf16)


def total_kernel(pieces_ref, out_ref):
    total = jnp.sum(pieces_ref[...].astype(f32), axis=0)
    size = out_ref.shape[0]
    for c in range(out_ref.shape[1] // BLK):
        out_ref[:, c * BLK : (c + 1) * BLK] = total[c * size : (c + 1) * size, :]


def shape(dims, dtype):
    return jax.ShapeDtypeStruct(dims, dtype)


def body(attn, weight, d_out):
    count, width = attn.shape
    features = weight.shape[0]
    group, near, far = lax.axis_size(TENSOR), lax.axis_size(NEAR), lax.axis_size(FAR)
    tall = lax.axis_size("yh")
    rows = count // group
    yh, core = lax.axis_index("yh"), lax.axis_index("core")
    odd = lax.rem(lax.axis_index("x"), 2)

    full_grad = lax.all_gather(d_out, TENSOR, axis=0, tiled=True)
    packed, full_grad = pack(attn, full_grad)
    packed, attn = lax.optimization_barrier((packed, attn))
    pieces = lax.all_to_all(packed, NEAR, 0, 0)

    (d_attn,) = call(
        d_attn_kernel, (shape((count, width), bf16),), (), full_grad, weight, flops=2 * count * features * width
    )
    attn, d_attn = lax.optimization_barrier((attn, d_attn))
    half = shape((tall, rows, features), bf16)
    keep, send = call(
        values_kernel, (half, half), (core,), attn, weight, flops=2 * count * features * (width + 3 * BLK)
    )
    arrived = lax.ppermute(send, "core", [(0, 1), (1, 0)])
    one = shape((rows, features), bf16)
    own, *sent = call(pair_kernel, (shape((rows, features), f32), one, one, one), (yh,), keep, arrived)

    pieces, sent, d_attn = lax.optimization_barrier((pieces, sent, d_attn))
    (plane,) = call(
        grad_kernel,
        (shape((far, features // near // far * width // BLK, BLK), bf16),),
        (odd,),
        pieces,
        flops=2 * near * count * WINDOW * width,
    )
    plane, sent = lax.optimization_barrier((plane, sent))
    terms = lax.all_to_all(plane, FAR, 0, 0)

    blocks = []
    for step in range(1, tall):
        blocks.append(lax.ppermute(sent[step - 1], "yh", [(i, (i + step) % tall) for i in range(tall)]))
    (mixed,) = call(mixed_kernel, (one,), (), own, *blocks)
    (w_grad,) = call(total_kernel, (shape((features // near // far, width), f32),), (), terms)
    return (mixed, d_attn, w_grad)


def solution(mesh):
    fine = Mesh(mesh.devices.reshape(2, 4, 16, 4, 2), ("yl", "x", "z", "yh", "core"))
    dp = ("yl", "x", "z")
    in_specs = (P(dp, TENSOR), P(None, TENSOR), P(dp + TENSOR, None))
    out_specs = (P(dp + TENSOR, None), P(dp, TENSOR), P(dp, TENSOR))
    return jax.shard_map(body, mesh=fine, in_specs=in_specs, out_specs=out_specs, check_vma=False)
```

```python
import jax
import jax.numpy as jnp
from jax import lax
from jax.experimental import pallas as pl
from jax.experimental.pallas import tpu as pltpu
from jax.sharding import Mesh
from jax.sharding import PartitionSpec as P

BLK = 128
TENSOR = ("yh", "core")
NEAR = ("yl", "x")
FAR = "z"
CHUNKS = 8
WINDOW = 384
VMEM_LIMIT = 16 * 1024 * 1024

code_offset = 6.0
bf16, f32 = jnp.bfloat16, jnp.float32


def call(kernel, outs, scalars, *arrays, flops=0):
    specs = [pl.BlockSpec(memory_space=pltpu.SMEM)] * len(scalars)
    specs += [pl.BlockSpec(memory_space=pltpu.VMEM)] * len(arrays)
    moved = sum(a.size * a.dtype.itemsize for a in tuple(arrays) + tuple(outs))
    return pl.pallas_call(
        kernel,
        out_shape=outs,
        in_specs=specs,
        out_specs=tuple(pl.BlockSpec(memory_space=pltpu.VMEM) for _ in outs),
        compiler_params=pltpu.CompilerParams(vmem_limit_bytes=VMEM_LIMIT),
        cost_estimate=pl.CostEstimate(flops=flops, bytes_accessed=moved, transcendentals=0),
    )(*[jnp.reshape(s, (1,)).astype(jnp.int32) for s in scalars], *arrays)


def signs_table():
    rows = lax.broadcasted_iota(jnp.int32, (BLK, BLK), 0)
    cols = lax.broadcasted_iota(jnp.int32, (BLK, BLK), 1)
    common = jnp.bitwise_and(rows, cols)
    parity = jnp.zeros((BLK, BLK), jnp.int32)
    for place in range(BLK.bit_length() - 1):
        parity = parity + jnp.bitwise_and(jnp.right_shift(common, place), 1)
    return (1 - 2 * jnp.bitwise_and(parity, 1)).astype(f32).astype(bf16)


def rotate(field, table):
    high = field.astype(bf16)
    rest = field - high.astype(f32)
    middle = rest.astype(bf16)
    low = (rest - middle.astype(f32)).astype(bf16)
    turned = jnp.dot(high, table, preferred_element_type=f32)
    turned += jnp.dot(middle, table, preferred_element_type=f32)
    turned += jnp.dot(low, table, preferred_element_type=f32)
    return turned * (BLK**-0.5)


def pack_kernel(attn_ref, d_ref, out_ref, grads_ref, attn_here, d_here, stage_a, stage_d, sems):
    count, width = attn_here.shape
    half = count // 2
    first = pltpu.make_async_copy(attn_ref, attn_here, sems.at[0])
    second = pltpu.make_async_copy(d_ref, d_here, sems.at[1])
    first.start()
    second.start()
    copies = []

    def send(source, target):
        copies.append(pltpu.make_async_copy(source, target, sems.at[2 + len(copies)]))
        copies[-1].start()

    first.wait()
    for c in range(width // BLK):
        stage_a[c * count : (c + 1) * count, :] = attn_here[:, c * BLK : (c + 1) * BLK]
    for i in range(CHUNKS):
        send(stage_a, out_ref.at[i, pl.ds(0, stage_a.shape[0]), :])
    second.wait()
    send(d_here, grads_ref)
    low = lax.broadcasted_iota(jnp.int32, (half, BLK), 1) < BLK // 2
    for i in range(CHUNKS):
        pair = i // 2 * 5 * BLK
        for k in range(2):
            start = pair + (3 * BLK if i % 2 else 0) + k * BLK
            stage_d[i, k * count : (k + 1) * count, :] = d_here[:, start : start + BLK]
        tile = d_here[:, pair + 2 * BLK : pair + 3 * BLK].astype(f32)
        top, bottom = tile[:half], tile[half:]
        if i % 2:
            fold = jnp.where(low, pltpu.roll(top, BLK // 2, 1), bottom)
        else:
            fold = jnp.where(low, top, pltpu.roll(bottom, BLK // 2, 1))
        stage_d[i, 2 * count :, :] = fold.astype(bf16)
        send(stage_d.at[i], out_ref.at[i, pl.ds(stage_a.shape[0], stage_d.shape[1]), :])
    for copy in copies:
        copy.wait()


def pack(attn, full_grad):
    (count, width), features = attn.shape, full_grad.shape[1]
    lines = (count * width // BLK, count * features // CHUNKS // BLK)
    return pl.pallas_call(
        pack_kernel,
        out_shape=(shape((CHUNKS, sum(lines), BLK), bf16), shape(full_grad.shape, bf16)),
        in_specs=[pl.BlockSpec(memory_space=pltpu.HBM)] * 2,
        out_specs=(pl.BlockSpec(memory_space=pltpu.HBM),) * 2,
        scratch_shapes=[
            pltpu.VMEM(attn.shape, bf16),
            pltpu.VMEM(full_grad.shape, bf16),
            pltpu.VMEM((lines[0], BLK), bf16),
            pltpu.VMEM((CHUNKS, lines[1], BLK), bf16),
            pltpu.SemaphoreType.DMA((3 + 2 * CHUNKS,)),
        ],
        cost_estimate=pl.CostEstimate(flops=0, bytes_accessed=10**7, transcendentals=0),
    )(attn, full_grad)


def values_kernel(core_ref, attn_ref, weight_ref, keep_ref, send_ref):
    table = signs_table()
    count, features = attn_ref.shape[0], weight_ref.shape[0]
    tall, rows = keep_ref.shape[0], keep_ref.shape[1]
    first = core_ref[0] == 0
    for j in range(features // BLK):
        cols = slice(j * BLK, (j + 1) * BLK)
        partial_value = lax.dot_general(
            attn_ref[...], weight_ref[cols, :], (((1,), (1,)), ((), ())), preferred_element_type=f32
        )
        turned = rotate(partial_value, table)
        top = jnp.max(jnp.abs(turned), axis=1, keepdims=True) + 1e-06
        scale = top.astype(bf16).astype(f32)
        coded = (turned / scale + code_offset).astype(bf16)
        values = ((coded.astype(f32) - code_offset) * scale).reshape(tall, 2, rows, BLK)
        zero, one = values[:, 0], values[:, 1]
        keep_ref[:, :, cols] = jnp.where(first, zero, one).astype(bf16)
        send_ref[:, :, cols] = jnp.where(first, one, zero).astype(bf16)


def pair_kernel(me_ref, keep_ref, arrived_ref, own_ref, *sent_refs):
    tall = keep_ref.shape[0]
    me = me_ref[0]
    own_ref[...] = keep_ref[me].astype(f32) + arrived_ref[me].astype(f32)
    for step in range(1, tall):
        other = lax.rem(me + step, tall)
        total = keep_ref[other].astype(f32) + arrived_ref[other].astype(f32)
        sent_refs[step - 1][...] = total.astype(bf16)


def mixed_kernel(own_ref, a_ref, b_ref, c_ref, out_ref):
    table = signs_table()
    for j in range(out_ref.shape[1] // BLK):
        cols = slice(j * BLK, (j + 1) * BLK)
        total = own_ref[:, cols] + a_ref[:, cols].astype(f32)
        total += b_ref[:, cols].astype(f32) + c_ref[:, cols].astype(f32)
        out_ref[:, cols] = rotate(total, table).astype(bf16)


def grad_kernel(odd_ref, near_ref, out_ref):
    far, size = out_ref.shape[0], out_ref.shape[1] * BLK // WINDOW
    near, count, tiles = near_ref.shape[0], BLK, WINDOW // BLK
    half = count // 2

    def piece(p, k):
        return near_ref[p, k * count : (k + 1) * count, :]

    def times(left, right):
        return lax.dot_general(left, right, (((0,), (0,)), ((), ())), preferred_element_type=f32)

    attns = [jnp.concatenate([piece(p, k) for k in range(tiles)], axis=1) for p in range(near)]
    whole = jnp.concatenate(
        [jnp.concatenate([piece(p, tiles), piece(p, tiles + 1)], axis=1) for p in range(near)], axis=0
    )
    whole = times(whole, jnp.concatenate(attns, axis=0))
    folds = jnp.concatenate([near_ref[p, (tiles + 2) * count :, :] for p in range(near)], axis=0)
    top = times(folds, jnp.concatenate([a[:half] for a in attns], axis=0))
    bottom = times(folds, jnp.concatenate([a[half:] for a in attns], axis=0))
    rest = top[: BLK // 2] + bottom[BLK // 2 :]
    even, odd = jnp.concatenate([whole, rest], axis=0), jnp.concatenate([rest, whole], axis=0)
    term = jnp.where(odd_ref[0] == 1, odd, even)
    for z in range(far):
        block = term[z * size : (z + 1) * size, :]
        parts = [block[:, c : c + BLK] for c in range(0, term.shape[1], BLK)]
        out_ref[z] = jnp.concatenate(parts, axis=0).astype(bf16)


def d_attn_kernel(d_ref, weight_ref, out_ref):
    product = jnp.dot(d_ref[...], weight_ref[...], preferred_element_type=f32)
    out_ref[...] = product.astype(bf16)


def total_kernel(pieces_ref, out_ref):
    total = jnp.sum(pieces_ref[...].astype(f32), axis=0)
    size = out_ref.shape[0]
    for c in range(out_ref.shape[1] // BLK):
        out_ref[:, c * BLK : (c + 1) * BLK] = total[c * size : (c + 1) * size, :]


def shape(dims, dtype):
    return jax.ShapeDtypeStruct(dims, dtype)


def body(attn, weight, d_out):
    count, width = attn.shape
    features = weight.shape[0]
    group, near, far = lax.axis_size(TENSOR), lax.axis_size(NEAR), lax.axis_size(FAR)
    tall = lax.axis_size("yh")
    rows = count // group
    yh, core = lax.axis_index("yh"), lax.axis_index("core")
    odd = lax.rem(lax.axis_index("x"), 2)

    full_grad = lax.all_gather(d_out, TENSOR, axis=0, tiled=True)
    packed, full_grad = pack(attn, full_grad)
    packed, attn = lax.optimization_barrier((packed, attn))
    pieces = lax.all_to_all(packed, NEAR, 0, 0)

    (d_attn,) = call(
        d_attn_kernel, (shape((count, width), bf16),), (), full_grad, weight, flops=2 * count * features * width
    )
    attn, d_attn = lax.optimization_barrier((attn, d_attn))
    half = shape((tall, rows, features), bf16)
    keep, send = call(
        values_kernel, (half, half), (core,), attn, weight, flops=2 * count * features * (width + 3 * BLK)
    )
    arrived = lax.ppermute(send, "core", [(0, 1), (1, 0)])
    one = shape((rows, features), bf16)
    own, *sent = call(pair_kernel, (shape((rows, features), f32), one, one, one), (yh,), keep, arrived)

    rings = [[(i, (i + step) % tall) for i in range(tall)] for step in range(tall)]
    first = lax.ppermute(sent[0], "yh", rings[1])
    pieces, first, later, d_attn = lax.optimization_barrier((pieces, first, sent[1:], d_attn))
    (plane,) = call(
        grad_kernel,
        (shape((far, features // near // far * width // BLK, BLK), bf16),),
        (odd,),
        pieces,
        flops=2 * near * count * WINDOW * width,
    )
    plane, later = lax.optimization_barrier((plane, later))
    terms = lax.all_to_all(plane, FAR, 0, 0)

    blocks = [first] + [lax.ppermute(later[step - 2], "yh", rings[step]) for step in range(2, tall)]
    (mixed,) = call(mixed_kernel, (one,), (), own, *blocks)
    (w_grad,) = call(total_kernel, (shape((features // near // far, width), f32),), (), terms)
    return (mixed, d_attn, w_grad)


def solution(mesh):
    fine = Mesh(mesh.devices.reshape(2, 4, 16, 4, 2), ("yl", "x", "z", "yh", "core"))
    dp = ("yl", "x", "z")
    in_specs = (P(dp, TENSOR), P(None, TENSOR), P(dp + TENSOR, None))
    out_specs = (P(dp + TENSOR, None), P(dp, TENSOR), P(dp, TENSOR))
    return jax.shard_map(body, mesh=fine, in_specs=in_specs, out_specs=out_specs, check_vma=False)
```

```python
import jax
import jax.numpy as jnp
from jax import lax
from jax.experimental import pallas as pl
from jax.experimental.pallas import tpu as pltpu
from jax.sharding import Mesh
from jax.sharding import PartitionSpec as P

BLK = 128
TENSOR = ("yh", "core")
NEAR = ("yl", "x")
FAR = "z"
CHUNKS = 8
WINDOW = 384
VMEM_LIMIT = 16 * 1024 * 1024

code_offset = 6.0
bf16, f32 = jnp.bfloat16, jnp.float32


def call(kernel, outs, scalars, *arrays, flops=0):
    specs = [pl.BlockSpec(memory_space=pltpu.SMEM)] * len(scalars)
    specs += [pl.BlockSpec(memory_space=pltpu.VMEM)] * len(arrays)
    moved = sum(a.size * a.dtype.itemsize for a in tuple(arrays) + tuple(outs))
    return pl.pallas_call(
        kernel,
        out_shape=outs,
        in_specs=specs,
        out_specs=tuple(pl.BlockSpec(memory_space=pltpu.VMEM) for _ in outs),
        compiler_params=pltpu.CompilerParams(vmem_limit_bytes=VMEM_LIMIT),
        cost_estimate=pl.CostEstimate(flops=flops, bytes_accessed=moved, transcendentals=0),
    )(*[jnp.reshape(s, (1,)).astype(jnp.int32) for s in scalars], *arrays)


def signs_table():
    rows = lax.broadcasted_iota(jnp.int32, (BLK, BLK), 0)
    cols = lax.broadcasted_iota(jnp.int32, (BLK, BLK), 1)
    common = jnp.bitwise_and(rows, cols)
    parity = jnp.zeros((BLK, BLK), jnp.int32)
    for place in range(BLK.bit_length() - 1):
        parity = parity + jnp.bitwise_and(jnp.right_shift(common, place), 1)
    return (1 - 2 * jnp.bitwise_and(parity, 1)).astype(f32).astype(bf16)


def rotate(field, table):
    high = field.astype(bf16)
    rest = field - high.astype(f32)
    middle = rest.astype(bf16)
    low = (rest - middle.astype(f32)).astype(bf16)
    turned = jnp.dot(high, table, preferred_element_type=f32)
    turned += jnp.dot(middle, table, preferred_element_type=f32)
    turned += jnp.dot(low, table, preferred_element_type=f32)
    return turned * (BLK**-0.5)


def pack_kernel(attn_ref, d_ref, out_ref, grads_ref, attn_here, d_here, stage_a, stage_d, sems):
    count, width = attn_here.shape
    half = count // 2
    first = pltpu.make_async_copy(attn_ref, attn_here, sems.at[0])
    second = pltpu.make_async_copy(d_ref, d_here, sems.at[1])
    first.start()
    second.start()
    copies = []

    def send(source, target):
        copies.append(pltpu.make_async_copy(source, target, sems.at[2 + len(copies)]))
        copies[-1].start()

    first.wait()
    for c in range(width // BLK):
        stage_a[c * count : (c + 1) * count, :] = attn_here[:, c * BLK : (c + 1) * BLK]
    for i in range(CHUNKS):
        send(stage_a, out_ref.at[i, pl.ds(0, stage_a.shape[0]), :])
    second.wait()
    send(d_here, grads_ref)
    low = lax.broadcasted_iota(jnp.int32, (half, BLK), 1) < BLK // 2
    for i in range(CHUNKS):
        pair = i // 2 * 5 * BLK
        for k in range(2):
            start = pair + (3 * BLK if i % 2 else 0) + k * BLK
            stage_d[i, k * count : (k + 1) * count, :] = d_here[:, start : start + BLK]
        tile = d_here[:, pair + 2 * BLK : pair + 3 * BLK].astype(f32)
        top, bottom = tile[:half], tile[half:]
        if i % 2:
            fold = jnp.where(low, pltpu.roll(top, BLK // 2, 1), bottom)
        else:
            fold = jnp.where(low, top, pltpu.roll(bottom, BLK // 2, 1))
        stage_d[i, 2 * count :, :] = fold.astype(bf16)
        send(stage_d.at[i], out_ref.at[i, pl.ds(stage_a.shape[0], stage_d.shape[1]), :])
    for copy in copies:
        copy.wait()


def pack(attn, full_grad):
    (count, width), features = attn.shape, full_grad.shape[1]
    lines = (count * width // BLK, count * features // CHUNKS // BLK)
    return pl.pallas_call(
        pack_kernel,
        out_shape=(shape((CHUNKS, sum(lines), BLK), bf16), shape(full_grad.shape, bf16)),
        in_specs=[pl.BlockSpec(memory_space=pltpu.HBM)] * 2,
        out_specs=(pl.BlockSpec(memory_space=pltpu.HBM),) * 2,
        scratch_shapes=[
            pltpu.VMEM(attn.shape, bf16),
            pltpu.VMEM(full_grad.shape, bf16),
            pltpu.VMEM((lines[0], BLK), bf16),
            pltpu.VMEM((CHUNKS, lines[1], BLK), bf16),
            pltpu.SemaphoreType.DMA((3 + 2 * CHUNKS,)),
        ],
        cost_estimate=pl.CostEstimate(flops=0, bytes_accessed=10**7, transcendentals=0),
    )(attn, full_grad)


def values_kernel(core_ref, attn_ref, weight_ref, keep_ref, send_ref):
    table = signs_table()
    count, features = attn_ref.shape[0], weight_ref.shape[0]
    tall, rows = keep_ref.shape[0], keep_ref.shape[1]
    first = core_ref[0] == 0
    for j in range(features // BLK):
        cols = slice(j * BLK, (j + 1) * BLK)
        partial_value = lax.dot_general(
            attn_ref[...], weight_ref[cols, :], (((1,), (1,)), ((), ())), preferred_element_type=f32
        )
        turned = rotate(partial_value, table)
        top = jnp.max(jnp.abs(turned), axis=1, keepdims=True) + 1e-06
        scale = top.astype(bf16).astype(f32)
        coded = (turned / scale + code_offset).astype(bf16)
        values = ((coded.astype(f32) - code_offset) * scale).reshape(tall, 2, rows, BLK)
        zero, one = values[:, 0], values[:, 1]
        keep_ref[:, :, cols] = jnp.where(first, zero, one).astype(bf16)
        send_ref[:, :, cols] = jnp.where(first, one, zero).astype(bf16)


def pair_kernel(me_ref, keep_ref, arrived_ref, own_ref, *sent_refs):
    tall = keep_ref.shape[0]
    me = me_ref[0]
    own_ref[...] = keep_ref[me].astype(f32) + arrived_ref[me].astype(f32)
    for step in range(1, tall):
        other = lax.rem(me + step, tall)
        total = keep_ref[other].astype(f32) + arrived_ref[other].astype(f32)
        sent_refs[step - 1][...] = total.astype(bf16)


def mixed_kernel(own_ref, a_ref, b_ref, c_ref, out_ref):
    table = signs_table()
    for j in range(out_ref.shape[1] // BLK):
        cols = slice(j * BLK, (j + 1) * BLK)
        total = own_ref[:, cols] + a_ref[:, cols].astype(f32)
        total += b_ref[:, cols].astype(f32) + c_ref[:, cols].astype(f32)
        out_ref[:, cols] = rotate(total, table).astype(bf16)


def grad_kernel(odd_ref, near_ref, out_ref):
    far, size = out_ref.shape[0], out_ref.shape[1] * BLK // WINDOW
    near, count, tiles = near_ref.shape[0], BLK, WINDOW // BLK
    half = count // 2

    def piece(p, k):
        return near_ref[p, k * count : (k + 1) * count, :]

    def times(left, right):
        return lax.dot_general(left, right, (((0,), (0,)), ((), ())), preferred_element_type=f32)

    attns = [jnp.concatenate([piece(p, k) for k in range(tiles)], axis=1) for p in range(near)]
    whole = jnp.concatenate(
        [jnp.concatenate([piece(p, tiles), piece(p, tiles + 1)], axis=1) for p in range(near)], axis=0
    )
    whole = times(whole, jnp.concatenate(attns, axis=0))
    folds = jnp.concatenate([near_ref[p, (tiles + 2) * count :, :] for p in range(near)], axis=0)
    top = times(folds, jnp.concatenate([a[:half] for a in attns], axis=0))
    bottom = times(folds, jnp.concatenate([a[half:] for a in attns], axis=0))
    rest = top[: BLK // 2] + bottom[BLK // 2 :]
    even, odd = jnp.concatenate([whole, rest], axis=0), jnp.concatenate([rest, whole], axis=0)
    term = jnp.where(odd_ref[0] == 1, odd, even)
    for z in range(far):
        block = term[z * size : (z + 1) * size, :]
        parts = [block[:, c : c + BLK] for c in range(0, term.shape[1], BLK)]
        out_ref[z] = jnp.concatenate(parts, axis=0).astype(bf16)


def d_attn_kernel(d_ref, weight_ref, out_ref):
    product = jnp.dot(d_ref[...], weight_ref[...], preferred_element_type=f32)
    out_ref[...] = product.astype(bf16)


def total_kernel(pieces_ref, out_ref):
    total = jnp.sum(pieces_ref[...].astype(f32), axis=0)
    size = out_ref.shape[0]
    for c in range(out_ref.shape[1] // BLK):
        out_ref[:, c * BLK : (c + 1) * BLK] = total[c * size : (c + 1) * size, :]


def shape(dims, dtype):
    return jax.ShapeDtypeStruct(dims, dtype)


def body(attn, weight, d_out):
    count, width = attn.shape
    features = weight.shape[0]
    group, near, far = lax.axis_size(TENSOR), lax.axis_size(NEAR), lax.axis_size(FAR)
    tall = lax.axis_size("yh")
    rows = count // group
    yh, core = lax.axis_index("yh"), lax.axis_index("core")
    odd = lax.rem(lax.axis_index("x"), 2)

    full_grad = lax.all_gather(d_out, TENSOR, axis=0, tiled=True)
    packed, full_grad = pack(attn, full_grad)
    packed, attn = lax.optimization_barrier((packed, attn))
    pieces = lax.all_to_all(packed, NEAR, 0, 0)

    (d_attn,) = call(
        d_attn_kernel, (shape((count, width), bf16),), (), full_grad, weight, flops=2 * count * features * width
    )
    attn, d_attn = lax.optimization_barrier((attn, d_attn))
    half = shape((tall, rows, features), bf16)
    keep, send = call(
        values_kernel, (half, half), (core,), attn, weight, flops=2 * count * features * (width + 3 * BLK)
    )
    arrived = lax.ppermute(send, "core", [(0, 1), (1, 0)])
    one = shape((rows, features), bf16)
    own, *sent = call(pair_kernel, (shape((rows, features), f32), one, one, one), (yh,), keep, arrived)

    pieces, sent, d_attn = lax.optimization_barrier((pieces, sent, d_attn))
    (plane,) = call(
        grad_kernel,
        (shape((far, features // near // far * width // BLK, BLK), bf16),),
        (odd,),
        pieces,
        flops=2 * near * count * WINDOW * width,
    )
    plane, sent = lax.optimization_barrier((plane, sent))
    terms = lax.all_to_all(plane, FAR, 0, 0)

    blocks = []
    for step in (2, 3, 1):
        blocks.append(lax.ppermute(sent[step - 1], "yh", [(i, (i + step) % tall) for i in range(tall)]))
    (mixed,) = call(mixed_kernel, (one,), (), own, *blocks)
    (w_grad,) = call(total_kernel, (shape((features // near // far, width), f32),), (), terms)
    return (mixed, d_attn, w_grad)


def solution(mesh):
    fine = Mesh(mesh.devices.reshape(2, 4, 16, 4, 2), ("yl", "x", "z", "yh", "core"))
    dp = ("yl", "x", "z")
    in_specs = (P(dp, TENSOR), P(None, TENSOR), P(dp + TENSOR, None))
    out_specs = (P(dp + TENSOR, None), P(dp, TENSOR), P(dp, TENSOR))
    return jax.shard_map(body, mesh=fine, in_specs=in_specs, out_specs=out_specs, check_vma=False)
```

```python
import jax
import jax.numpy as jnp
from jax import lax
from jax.experimental import pallas as pl
from jax.experimental.pallas import tpu as pltpu
from jax.sharding import Mesh
from jax.sharding import PartitionSpec as P

BLK = 128
TENSOR = ("yh", "core")
NEAR = ("yl", "x")
FAR = "z"
CHUNKS = 8
WINDOW = 384
VMEM_LIMIT = 16 * 1024 * 1024

code_offset = 6.0
bf16, f32 = jnp.bfloat16, jnp.float32


def call(kernel, outs, scalars, *arrays, flops=0):
    specs = [pl.BlockSpec(memory_space=pltpu.SMEM)] * len(scalars)
    specs += [pl.BlockSpec(memory_space=pltpu.VMEM)] * len(arrays)
    moved = sum(a.size * a.dtype.itemsize for a in tuple(arrays) + tuple(outs))
    return pl.pallas_call(
        kernel,
        out_shape=outs,
        in_specs=specs,
        out_specs=tuple(pl.BlockSpec(memory_space=pltpu.VMEM) for _ in outs),
        compiler_params=pltpu.CompilerParams(vmem_limit_bytes=VMEM_LIMIT),
        cost_estimate=pl.CostEstimate(flops=flops, bytes_accessed=moved, transcendentals=0),
    )(*[jnp.reshape(s, (1,)).astype(jnp.int32) for s in scalars], *arrays)


def signs_table():
    rows = lax.broadcasted_iota(jnp.int32, (BLK, BLK), 0)
    cols = lax.broadcasted_iota(jnp.int32, (BLK, BLK), 1)
    common = jnp.bitwise_and(rows, cols)
    parity = jnp.zeros((BLK, BLK), jnp.int32)
    for place in range(BLK.bit_length() - 1):
        parity = parity + jnp.bitwise_and(jnp.right_shift(common, place), 1)
    return (1 - 2 * jnp.bitwise_and(parity, 1)).astype(f32).astype(bf16)


def rotate(field, table):
    high = field.astype(bf16)
    rest = field - high.astype(f32)
    middle = rest.astype(bf16)
    low = (rest - middle.astype(f32)).astype(bf16)
    turned = jnp.dot(high, table, preferred_element_type=f32)
    turned += jnp.dot(middle, table, preferred_element_type=f32)
    turned += jnp.dot(low, table, preferred_element_type=f32)
    return turned * (BLK**-0.5)


def pack_kernel(attn_ref, d_ref, out_ref, grads_ref, attn_here, d_here, stage_a, stage_d, sems):
    count, width = attn_here.shape
    half = count // 2
    first = pltpu.make_async_copy(attn_ref, attn_here, sems.at[0])
    second = pltpu.make_async_copy(d_ref, d_here, sems.at[1])
    first.start()
    second.start()
    copies = []

    def send(source, target):
        copies.append(pltpu.make_async_copy(source, target, sems.at[2 + len(copies)]))
        copies[-1].start()

    first.wait()
    for c in range(width // BLK):
        stage_a[c * count : (c + 1) * count, :] = attn_here[:, c * BLK : (c + 1) * BLK]
    for i in range(CHUNKS):
        send(stage_a, out_ref.at[i, pl.ds(0, stage_a.shape[0]), :])
    second.wait()
    send(d_here, grads_ref)
    low = lax.broadcasted_iota(jnp.int32, (half, BLK), 1) < BLK // 2
    for i in range(CHUNKS):
        pair = i // 2 * 5 * BLK
        for k in range(2):
            start = pair + (3 * BLK if i % 2 else 0) + k * BLK
            stage_d[i, k * count : (k + 1) * count, :] = d_here[:, start : start + BLK]
        tile = d_here[:, pair + 2 * BLK : pair + 3 * BLK].astype(f32)
        top, bottom = tile[:half], tile[half:]
        if i % 2:
            fold = jnp.where(low, pltpu.roll(top, BLK // 2, 1), bottom)
        else:
            fold = jnp.where(low, top, pltpu.roll(bottom, BLK // 2, 1))
        stage_d[i, 2 * count :, :] = fold.astype(bf16)
        send(stage_d.at[i], out_ref.at[i, pl.ds(stage_a.shape[0], stage_d.shape[1]), :])
    for copy in copies:
        copy.wait()


def pack(attn, full_grad):
    (count, width), features = attn.shape, full_grad.shape[1]
    lines = (count * width // BLK, count * features // CHUNKS // BLK)
    return pl.pallas_call(
        pack_kernel,
        out_shape=(shape((CHUNKS, sum(lines), BLK), bf16), shape(full_grad.shape, bf16)),
        in_specs=[pl.BlockSpec(memory_space=pltpu.HBM)] * 2,
        out_specs=(pl.BlockSpec(memory_space=pltpu.HBM),) * 2,
        scratch_shapes=[
            pltpu.VMEM(attn.shape, bf16),
            pltpu.VMEM(full_grad.shape, bf16),
            pltpu.VMEM((lines[0], BLK), bf16),
            pltpu.VMEM((CHUNKS, lines[1], BLK), bf16),
            pltpu.SemaphoreType.DMA((3 + 2 * CHUNKS,)),
        ],
        cost_estimate=pl.CostEstimate(flops=0, bytes_accessed=10**7, transcendentals=0),
    )(attn, full_grad)


def values_kernel(core_ref, attn_ref, weight_ref, keep_ref, send_ref):
    table = signs_table()
    count, features = attn_ref.shape[0], weight_ref.shape[0]
    tall, rows = keep_ref.shape[0], keep_ref.shape[1]
    first = core_ref[0] == 0
    for j in range(features // BLK):
        cols = slice(j * BLK, (j + 1) * BLK)
        partial_value = lax.dot_general(
            attn_ref[...], weight_ref[cols, :], (((1,), (1,)), ((), ())), preferred_element_type=f32
        )
        turned = rotate(partial_value, table)
        top = jnp.max(jnp.abs(turned), axis=1, keepdims=True) + 1e-06
        scale = top.astype(bf16).astype(f32)
        coded = (turned / scale + code_offset).astype(bf16)
        values = ((coded.astype(f32) - code_offset) * scale).reshape(tall, 2, rows, BLK)
        zero, one = values[:, 0], values[:, 1]
        keep_ref[:, :, cols] = jnp.where(first, zero, one).astype(bf16)
        send_ref[:, :, cols] = jnp.where(first, one, zero).astype(bf16)


def pair_kernel(me_ref, keep_ref, arrived_ref, own_ref, *sent_refs):
    tall = keep_ref.shape[0]
    me = me_ref[0]
    own_ref[...] = keep_ref[me].astype(f32) + arrived_ref[me].astype(f32)
    for step in range(1, tall):
        other = lax.rem(me + step, tall)
        total = keep_ref[other].astype(f32) + arrived_ref[other].astype(f32)
        sent_refs[step - 1][...] = total.astype(bf16)


def mixed_kernel(own_ref, a_ref, b_ref, c_ref, out_ref):
    rows, features = out_ref.shape
    total = own_ref[...] + a_ref[...].astype(f32)
    total += b_ref[...].astype(f32) + c_ref[...].astype(f32)
    blocks = [total[:, c : c + BLK] for c in range(0, features, BLK)]
    turned = rotate(jnp.concatenate(blocks, axis=0), signs_table()).astype(bf16)
    for j in range(features // BLK):
        out_ref[:, j * BLK : (j + 1) * BLK] = turned[j * rows : (j + 1) * rows, :]


def grad_kernel(odd_ref, near_ref, out_ref):
    far, size = out_ref.shape[0], out_ref.shape[1] * BLK // WINDOW
    near, count, tiles = near_ref.shape[0], BLK, WINDOW // BLK
    half = count // 2

    def piece(p, k):
        return near_ref[p, k * count : (k + 1) * count, :]

    def times(left, right):
        return lax.dot_general(left, right, (((0,), (0,)), ((), ())), preferred_element_type=f32)

    attns = [jnp.concatenate([piece(p, k) for k in range(tiles)], axis=1) for p in range(near)]
    whole = jnp.concatenate(
        [jnp.concatenate([piece(p, tiles), piece(p, tiles + 1)], axis=1) for p in range(near)], axis=0
    )
    whole = times(whole, jnp.concatenate(attns, axis=0))
    folds = jnp.concatenate([near_ref[p, (tiles + 2) * count :, :] for p in range(near)], axis=0)
    top = times(folds, jnp.concatenate([a[:half] for a in attns], axis=0))
    bottom = times(folds, jnp.concatenate([a[half:] for a in attns], axis=0))
    rest = top[: BLK // 2] + bottom[BLK // 2 :]
    even, odd = jnp.concatenate([whole, rest], axis=0), jnp.concatenate([rest, whole], axis=0)
    term = jnp.where(odd_ref[0] == 1, odd, even)
    for z in range(far):
        block = term[z * size : (z + 1) * size, :]
        parts = [block[:, c : c + BLK] for c in range(0, term.shape[1], BLK)]
        out_ref[z] = jnp.concatenate(parts, axis=0).astype(bf16)


def d_attn_kernel(d_ref, weight_ref, out_ref):
    product = jnp.dot(d_ref[...], weight_ref[...], preferred_element_type=f32)
    out_ref[...] = product.astype(bf16)


def total_kernel(pieces_ref, out_ref):
    total = jnp.sum(pieces_ref[...].astype(f32), axis=0)
    size = out_ref.shape[0]
    for c in range(out_ref.shape[1] // BLK):
        out_ref[:, c * BLK : (c + 1) * BLK] = total[c * size : (c + 1) * size, :]


def shape(dims, dtype):
    return jax.ShapeDtypeStruct(dims, dtype)


def body(attn, weight, d_out):
    count, width = attn.shape
    features = weight.shape[0]
    group, near, far = lax.axis_size(TENSOR), lax.axis_size(NEAR), lax.axis_size(FAR)
    tall = lax.axis_size("yh")
    rows = count // group
    yh, core = lax.axis_index("yh"), lax.axis_index("core")
    odd = lax.rem(lax.axis_index("x"), 2)

    full_grad = lax.all_gather(d_out, TENSOR, axis=0, tiled=True)
    packed, full_grad = pack(attn, full_grad)
    packed, attn = lax.optimization_barrier((packed, attn))
    pieces = lax.all_to_all(packed, NEAR, 0, 0)

    (d_attn,) = call(
        d_attn_kernel, (shape((count, width), bf16),), (), full_grad, weight, flops=2 * count * features * width
    )
    attn, d_attn = lax.optimization_barrier((attn, d_attn))
    half = shape((tall, rows, features), bf16)
    keep, send = call(
        values_kernel, (half, half), (core,), attn, weight, flops=2 * count * features * (width + 3 * BLK)
    )
    arrived = lax.ppermute(send, "core", [(0, 1), (1, 0)])
    one = shape((rows, features), bf16)
    own, *sent = call(pair_kernel, (shape((rows, features), f32), one, one, one), (yh,), keep, arrived)

    pieces, sent, d_attn = lax.optimization_barrier((pieces, sent, d_attn))
    (plane,) = call(
        grad_kernel,
        (shape((far, features // near // far * width // BLK, BLK), bf16),),
        (odd,),
        pieces,
        flops=2 * near * count * WINDOW * width,
    )
    plane, sent = lax.optimization_barrier((plane, sent))
    terms = lax.all_to_all(plane, FAR, 0, 0)

    blocks = []
    for step in (2, 3, 1):
        blocks.append(lax.ppermute(sent[step - 1], "yh", [(i, (i + step) % tall) for i in range(tall)]))
    (mixed,) = call(mixed_kernel, (one,), (), own, *blocks)
    (w_grad,) = call(total_kernel, (shape((features // near // far, width), f32),), (), terms)
    return (mixed, d_attn, w_grad)


def solution(mesh):
    fine = Mesh(mesh.devices.reshape(2, 4, 16, 4, 2), ("yl", "x", "z", "yh", "core"))
    dp = ("yl", "x", "z")
    in_specs = (P(dp, TENSOR), P(None, TENSOR), P(dp + TENSOR, None))
    out_specs = (P(dp + TENSOR, None), P(dp, TENSOR), P(dp, TENSOR))
    return jax.shard_map(body, mesh=fine, in_specs=in_specs, out_specs=out_specs, check_vma=False)
```
